512 devices in a mesh: row: 32 (over z, core), col: 16 (over y, x).
Axes of the slice: x: 4, y: 4, z: 16, core: 2. Of those that a mesh axis runs over, the one named last changes fastest.
Arguments:
- z_slab: float32 [98304, 2048], P('row', 'col'), may hold values from -6 to 6
- v_first: float32 [98304, 256], P('row', 'col'), may hold values from -0.01953125 to 0.01953125
- v_second: float32 [98304, 256], P('row', 'col'), may hold values from -0.01953125 to 0.01953125
- t_first: float32 [256, 256], replicated, may hold values from -2.4 to 2.4, as said below
- t_second: float32 [256, 256], replicated, may hold values from -2.4 to 2.4, as said below
Outputs:
- z_result: float32 [98304, 2048], P('row', 'col')
The draws below stay inside these ranges and needn't reach their ends.
Inputs may be any that keep to these rules, and one draw needn't show every extreme that they name: `t_first`: upper triangular; diagonal entries lie in 1.5 to 2. `t_second`: upper triangular; diagonal entries lie in 1.5 to 2.
All inputs are finite; a program needn't handle non-finite values.
Results may differ from the reference program's by a relative error of at most 0.00011.
Values sent between devices are 32-bit elements; how exact they have to be, the bound alone decides.
No kernel may reach another device: no remote copies, remote signals or barrier semaphores. Data moves between devices by JAX's collectives and lax.ppermute only.
A program may use at most 64 MiB of HBM per device.

```python
import jax
import jax.numpy as jnp
from jax import lax

N = 98304
M = 2048
K = 256


def triangle(key, low, high, spread):
    key_diag, key_off = jax.random.split(key)
    diag_vals = jax.random.uniform(key_diag, (K,), jnp.float32, 1.5, 2.0)
    off_vals = jnp.clip(jax.random.normal(key_off, (K, K), jnp.float32) * spread, low, high)
    return jnp.triu(off_vals, 1) + jnp.diag(diag_vals)


def draw_t_first(key, part):
    key = jax.random.fold_in(key, 11)
    return triangle(key, -2.4, 2.4, 0.4)


def draw_t_second(key, part):
    key = jax.random.fold_in(key, 23)
    return triangle(key, -2.4, 2.4, 0.4)


def shard_levels(stream_key, shape, cuts, low, high):
    loudness = 1.0
    for position, shards_of in cuts:
        draws = jax.random.uniform(jax.random.fold_in(jax.random.fold_in(stream_key, 6), position), (shards_of,), jnp.float32, low / len(cuts), high / len(cuts))
        loudness = loudness * jnp.repeat(jnp.exp(draws), shape[position] // shards_of).reshape((-1,) + (1,) * (len(shape) - 1 - position))
    return loudness


def scatter_about(key, dims, deviation, reach, cuts=(), dtype=jnp.bfloat16):
    values = deviation * jax.random.normal(key, dims, jnp.float32)
    if cuts:
        values = values * shard_levels(key, dims, cuts, -0.22, 0.18)
    return jnp.clip(values, -reach, reach).astype(dtype)


def setup_inputs(seed: int = 0) -> dict:
    streams_of = jax.random.split(jax.random.key(seed), 6)
    z_slab = scatter_about(streams_of[0], (N, M), 1.0, 6.0, ((0, 32), (1, 16)), jnp.float32)
    v_first = scatter_about(streams_of[1], (N, K), N ** -0.5, 0.01953125, ((0, 32), (1, 16)), jnp.float32)
    v_second = scatter_about(streams_of[2], (N, K), N ** -0.5, 0.01953125, ((0, 32), (1, 16)), jnp.float32)
    t_first = draw_t_first(jax.random.fold_in(streams_of[5], 71), 0)
    t_second = draw_t_second(jax.random.fold_in(streams_of[5], 71), 0)
    return {"z_slab": z_slab, "v_first": v_first, "v_second": v_second, "t_first": t_first, "t_second": t_second}


def product(left, right):
    return jnp.dot(left, right, precision=lax.Precision.HIGHEST, preferred_element_type=jnp.float32)


def project(vectors, slab):
    return jnp.einsum("nk,nm->km", vectors, slab, precision=lax.Precision.HIGHEST, preferred_element_type=jnp.float32)


def reference(z_slab, v_first, v_second, t_first, t_second):
    coeff_second = project(v_second, z_slab)
    z_mid = z_slab - product(v_second, product(t_second, coeff_second))
    coeff_first = project(v_first, z_mid)
    return z_mid - product(v_first, product(t_first, coeff_first))
```

```python
import jax
import jax.numpy as jnp
from jax import lax
from jax.sharding import PartitionSpec as P

NEAR = 8
FAR = 4
HIGHEST = lax.Precision.HIGHEST


def product(left, right):
    return jnp.dot(left, right, precision=HIGHEST, preferred_element_type=jnp.float32)


def sum_over_row(part):
    near = [[NEAR * g + i for i in range(NEAR)] for g in range(FAR)]
    far = [[i + NEAR * g for g in range(FAR)] for i in range(NEAR)]
    r, m = part.shape
    blocks = lax.all_to_all(part.reshape(NEAR, r // NEAR, m), "row", 0, 0, axis_index_groups=near, tiled=True)
    mine = jnp.sum(blocks, 0)
    far_blocks = lax.all_to_all(
        jnp.broadcast_to(mine[None], (FAR,) + mine.shape), "row", 0, 0, axis_index_groups=far, tiled=True
    )
    mine = jnp.sum(far_blocks, 0)
    full = lax.all_to_all(
        jnp.broadcast_to(mine[None], (NEAR,) + mine.shape), "row", 0, 0, axis_index_groups=near, tiled=True
    )
    return full.reshape(r, m)


def body(z_slab, v_first, v_second, t_first, t_second):
    n, w = v_first.shape
    m = z_slab.shape[1]
    k = t_first.shape[0]
    own = jnp.stack([v_first.T, v_second.T])
    panels = lax.all_gather(own, "col", axis=1, tiled=True)
    panel_one, panel_two = panels[0], panels[1]
    coeffs = jnp.einsum("kn,nm->km", panels.reshape(2 * k, n), z_slab, precision=HIGHEST)
    gram = jnp.einsum("kn,jn->kj", panel_one, panel_two, precision=HIGHEST)
    stacked = jnp.concatenate([coeffs, gram[:, :m], gram[:, m:]], 0)
    total = sum_over_row(stacked)
    gram = jnp.concatenate([total[2 * k : 3 * k], total[3 * k :]], 1)
    x_two = product(t_second, total[k : 2 * k])
    x_one = product(t_first, total[:k] - product(gram, x_two))
    x = jnp.concatenate([x_one, x_two], 0)
    return z_slab - jnp.einsum("kn,km->nm", panels.reshape(2 * k, n), x, precision=HIGHEST)


def solution(mesh):
    placed = (P("row", "col"), P("row", "col"), P("row", "col"), P(), P())
    return jax.shard_map(
        body, mesh=mesh, in_specs=placed, out_specs=P("row", "col"), check_vma=False
    )
```

```python
import functools

import jax
import jax.numpy as jnp
from jax import lax
from jax.experimental import pallas as pl
from jax.experimental.pallas import tpu as pltpu
from jax.sharding import PartitionSpec as P

F32 = jnp.float32
BF16 = jnp.bfloat16
LANES = 128
XA, XB, YA, YB = 1, 3, 4, 12
SHARES = (7, 6, 6, 5)
PAIRS = 2
NEAR = 4
FAR = 4


def dot(left, right):
    return jnp.dot(left, right, preferred_element_type=F32)


def dot_t(left, right):
    return lax.dot_general(left, right, (((1,), (1,)), ((), ())), preferred_element_type=F32)


def exact(left, right):
    return jnp.dot(left, right, precision=lax.Precision.HIGHEST, preferred_element_type=F32)


def split(x):
    high = x.astype(BF16)
    return high, (x - high.astype(F32)).astype(BF16)


def swap(x, mask, size):
    return lax.ppermute(x, "col", [(i, i ^ mask) for i in range(size)])


def in_order(refs, masks, which, width):
    place = {}
    for ref, held in zip(refs, masks):
        for i, mask in enumerate(held):
            place[mask] = ref[which, i * width : (i + 1) * width, :]
    return jnp.concatenate([place[mask] for mask in sorted(place)], 0)


def project_kernel(masks, width, base, has_acc, *refs):
    refs = list(refs)
    acc_ref = refs.pop(0) if has_acc else None
    a_ref, b_ref, z_ref, out_ref = refs
    k = width * (len(masks[0]) + len(masks[1]))
    n = a_ref.shape[2]
    one_h, one_l = split(in_order((a_ref, b_ref), masks, 0, width))
    two_h, two_l = split(in_order((a_ref, b_ref), masks, 1, width))
    z_h, z_l = split(z_ref[base : base + n, :])
    z_both = jnp.concatenate([z_h, z_l], 1)
    m = z_h.shape[1]
    for row, high, low in ((0, one_h, one_l), (k, two_h, two_l)):
        wide = dot(high, z_both)
        part = wide[:, :m] + (wide[:, m:] + dot(low, z_h))
        if has_acc:
            part = part + acc_ref[row : row + k, :]
        out_ref[row : row + k, :] = part
    gram = dot_t(one_h, two_h) + (dot_t(one_h, two_l) + dot_t(one_l, two_h))
    for i in range(k // m):
        part = gram[:, i * m : (i + 1) * m]
        row = 2 * k + i * k
        if has_acc:
            part = part + acc_ref[row : row + k, :]
        out_ref[row : row + k, :] = part


def project(acc, piece, masks, z, base, k, width):
    m = z.shape[1]
    rows = 2 * k + k * k // m
    args = ([] if acc is None else [acc]) + list(piece) + [z]
    return pl.pallas_call(
        functools.partial(project_kernel, masks, width, base, acc is not None),
        out_shape=jax.ShapeDtypeStruct((rows, m), F32),
        in_specs=[pl.BlockSpec(memory_space=pltpu.VMEM)] * len(args),
        out_specs=pl.BlockSpec(memory_space=pltpu.VMEM),
        compiler_params=pltpu.CompilerParams(vmem_limit_bytes=32 << 20),
    )(*args)


def apply_kernel(all_masks, width, bases, col_ref, total_ref, t_one_ref, t_two_ref, z_ref, *refs):
    pieces, out_ref, true_ref, slot_ref = refs[:-3], refs[-3], refs[-2], refs[-1]
    k = t_one_ref.shape[0]
    m = z_ref.shape[1]
    blocks = k // width
    col = col_ref[0]

    def place(s):
        return pl.ds(pl.multiple_of(lax.bitwise_xor(col, s) * width, width), width)

    def solve(t_ref, coeff, row):
        for s in range(blocks):
            true_ref[place(s), :] = coeff[s * width : (s + 1) * width, :]
        true_ref[...] = exact(t_ref[...], true_ref[...])
        for s in range(blocks):
            slot_ref[row + s * width : row + (s + 1) * width, :] = true_ref[place(s), :]

    solve(t_two_ref, total_ref[k : 2 * k, :], k)
    coeff = total_ref[:k, :]
    for i in range(k // m):
        row = 2 * k + i * k
        coeff = coeff - exact(total_ref[row : row + k, :], slot_ref[k + i * m : k + (i + 1) * m, :])
    solve(t_one_ref, coeff, 0)
    x_h, x_l = split(slot_ref[...].T)
    x_both = jnp.concatenate([x_h, x_l], 0)
    for p, (base, masks) in enumerate(zip(bases, all_masks)):
        pair = pieces[2 * p : 2 * p + 2]
        n = pair[0].shape[2]
        both = jnp.concatenate([in_order(pair, masks, 0, width), in_order(pair, masks, 1, width)], 0)
        high, low = split(both)
        wide = dot(x_both, high)
        moved = wide[:m, :] + (wide[m:, :] + dot(x_h, low))
        out_ref[base : base + n, :] = z_ref[base : base + n, :] - moved.T


def apply(col, total, t_one, t_two, z, pieces, all_masks, bases, width):
    flat = [half for piece in pieces for half in piece]
    k = t_one.shape[0]
    vmem = pl.BlockSpec(memory_space=pltpu.VMEM)
    return pl.pallas_call(
        functools.partial(apply_kernel, all_masks, width, bases),
        out_shape=jax.ShapeDtypeStruct(z.shape, F32),
        in_specs=[pl.BlockSpec(memory_space=pltpu.SMEM)] + [vmem] * (4 + len(flat)),
        out_specs=vmem,
        scratch_shapes=[pltpu.VMEM((k, z.shape[1]), F32), pltpu.VMEM((2 * k, z.shape[1]), F32)],
        compiler_params=pltpu.CompilerParams(vmem_limit_bytes=40 << 20),
    )(col, total, t_one, t_two, z, *flat)


def gather_pieces(own, size):
    n = own.shape[2]
    unit = n // sum(SHARES)
    cuts = [unit * sum(SHARES[:i]) for i in range(len(SHARES) + 1)]

    def widen(held, mask):
        data, masks = held
        got = swap(data, mask, size)
        return jnp.concatenate([data, got], 1), masks + [m ^ mask for m in masks]

    def part(held, low, high):
        return held[0][:, :, low:high], held[1]

    first = (own[:, :, : cuts[2]], [0])
    second = (own[:, :, cuts[2] :], [0])
    first, second = widen(first, XA), widen(second, YA)
    first, second = widen(first, XB), widen(second, YB)
    parts = [
        (part(first, 0, cuts[1]), YA, YB),
        (part(first, cuts[1], cuts[2]), YB, YA),
        (part(second, 0, cuts[3] - cuts[2]), XA, XB),
        (part(second, cuts[3] - cuts[2], cuts[4] - cuts[2]), XB, XA),
    ]
    parts = [(widen(held, near), last) for held, near, last in parts]
    pieces, masks = [], []
    for (data, held), last in parts:
        pieces.append((data, swap(data, last, size)))
        masks.append((held, [m ^ last for m in held]))
    return pieces, masks, cuts


def sum_over_row(part):
    r, m = part.shape
    group = PAIRS * NEAR
    rows = group * FAR
    pair = [(i, i ^ 1) for i in range(rows)]
    near = [[group * g + PAIRS * i + c for i in range(NEAR)] for g in range(FAR) for c in range(PAIRS)]
    far = [[i + group * g for g in range(FAR)] for i in range(group)]
    core = lax.axis_index("row") % PAIRS
    half = r // PAIRS
    kept = lax.dynamic_slice_in_dim(part, core * half, half, 0)
    given = lax.dynamic_slice_in_dim(part, (1 - core) * half, half, 0)
    mine = kept + lax.ppermute(given, "row", pair)
    blocks = lax.all_to_all(mine.reshape(NEAR, half // NEAR, m), "row", 0, 0, axis_index_groups=near, tiled=True)
    mine = jnp.sum(blocks, 0)
    blocks = lax.all_to_all(
        jnp.broadcast_to(mine[None], (FAR,) + mine.shape), "row", 0, 0, axis_index_groups=far, tiled=True
    )
    mine = jnp.sum(blocks, 0)
    blocks = lax.all_to_all(
        jnp.broadcast_to(mine[None], (NEAR,) + mine.shape), "row", 0, 0, axis_index_groups=near, tiled=True
    )
    mine = blocks.reshape(half, m)
    other = lax.ppermute(mine, "row", pair)
    return jnp.where(core == 0, jnp.concatenate([mine, other], 0), jnp.concatenate([other, mine], 0))


def body(size, z_slab, v_first, v_second, t_first, t_second):
    n, width = v_first.shape
    k = t_first.shape[0]
    own = jnp.stack([v_first.T, v_second.T])
    pieces, masks, cuts = gather_pieces(own, size)
    part = None
    for piece, held, base in zip(pieces, masks, cuts):
        part = project(part, piece, held, z_slab, base, k, width)
    total = sum_over_row(part)
    col = lax.axis_index("col").astype(jnp.int32).reshape(1)
    return apply(col, total, t_first, t_second, z_slab, pieces, masks, cuts[:-1], width)


def solution(mesh):
    placed = (P("row", "col"), P("row", "col"), P("row", "col"), P(), P())
    return jax.shard_map(
        functools.partial(body, mesh.shape["col"]),
        mesh=mesh,
        in_specs=placed,
        out_specs=P("row", "col"),
        check_vma=False,
    )
```

```python
import functools

import jax
import jax.numpy as jnp
from jax import lax
from jax.experimental import pallas as pl
from jax.experimental.pallas import tpu as pltpu
from jax.sharding import PartitionSpec as P

F32 = jnp.float32
BF16 = jnp.bfloat16
LANES = 128
XA, XB, YA, YB = 1, 3, 4, 12
SHARES = (7, 5, 7, 5)
PAIRS = 2
NEAR = 4
FAR = 4
EARLY_VMEM = 24 << 20
LATE_VMEM = 16 << 20
APPLY_VMEM = 24 << 20


def dot(left, right):
    return jnp.dot(left, right, preferred_element_type=F32)


def dot_t(left, right):
    return lax.dot_general(left, right, (((1,), (1,)), ((), ())), preferred_element_type=F32)


def exact(left, right):
    return jnp.dot(left, right, precision=lax.Precision.HIGHEST, preferred_element_type=F32)


def split(x):
    high = x.astype(BF16)
    return high, (x - high.astype(F32)).astype(BF16)


def swap(x, mask, size):
    return lax.ppermute(x, "col", [(i, i ^ mask) for i in range(size)])


def in_order(pair, masks, row, width):
    blocks = {}
    for half, held in zip(pair, masks):
        for i, mask in enumerate(held):
            low = row * len(held) * width + i * width
            blocks[mask] = half[low : low + width, :]
    return jnp.concatenate([blocks[mask] for mask in sorted(blocks)], 0)


def scatter_rows(part, held, k, width):
    count = len(held)
    for which in range(2):
        for i, mask in enumerate(held):
            low = (which * count + i) * width
            yield which * k + mask * width, part[low : low + width, :]


def split_half(ref, high_ref, low_ref):
    rows = ref.shape[1]
    for which in range(2):
        high, low = split(ref[which])
        high_ref[which * rows : (which + 1) * rows, :] = high
        low_ref[which * rows : (which + 1) * rows, :] = low


def half_coeffs(high, low, z_both):
    m = z_both.shape[1] // 2
    wide = dot(high, z_both)
    return wide[:, :m] + (wide[:, m:] + dot(low, z_both[:, :m]))


def early_kernel(all_masks, width, bases, k, z_ref, *refs):
    count = len(bases)
    halves, acc_ref, zb_ref, out = refs[:count], refs[count], refs[count + 1], refs[count + 2 :]
    m = z_ref.shape[1]
    acc_ref[...] = jnp.zeros_like(acc_ref)
    for p, base in enumerate(bases):
        n = halves[p].shape[2]
        z_h, z_l = split(z_ref[base : base + n, :])
        zb_ref[base : base + n, :m] = z_h
        zb_ref[base : base + n, m:] = z_l
        split_half(halves[p], out[2 * p], out[2 * p + 1])
        part = half_coeffs(out[2 * p][...], out[2 * p + 1][...], zb_ref[base : base + n, :])
        for place, rows in scatter_rows(part, all_masks[p][0], k, width):
            acc_ref[place : place + width, :] += rows


def split_shapes(half):
    shape = jax.ShapeDtypeStruct((half.shape[0] * half.shape[1], half.shape[2]), BF16)
    return [shape, shape]


def vmem_specs(count):
    return [pl.BlockSpec(memory_space=pltpu.VMEM)] * count


def early(z, halves, all_masks, bases, k, width):
    n, m = z.shape
    shapes = [jax.ShapeDtypeStruct((2 * k, m), F32), jax.ShapeDtypeStruct((n, 2 * m), BF16)]
    for half in halves:
        shapes += split_shapes(half)
    out = pl.pallas_call(
        functools.partial(early_kernel, all_masks, width, bases, k),
        out_shape=shapes,
        in_specs=vmem_specs(1 + len(halves)),
        out_specs=vmem_specs(len(shapes)),
        compiler_params=pltpu.CompilerParams(vmem_limit_bytes=EARLY_VMEM),
        cost_estimate=pl.CostEstimate(flops=6 * k * n * m, bytes_accessed=12 << 20, transcendentals=0),
    )(z, *halves)
    return out[0], out[1], [(out[2 + 2 * p], out[3 + 2 * p]) for p in range(len(halves))]


def late_kernel(masks, width, base, k, first, acc_ref, got_ref, first_h, first_l, zb_ref, out_ref, got_h, got_l):
    n = got_ref.shape[2]
    m = zb_ref.shape[1] // 2
    split_half(got_ref, got_h, got_l)
    part = half_coeffs(got_h[...], got_l[...], zb_ref[base : base + n, :])
    added = {place: rows for place, rows in scatter_rows(part, masks[1], k, width)}
    for place in range(0, 2 * k, width):
        rows = acc_ref[place : place + width, :]
        out_ref[place : place + width, :] = rows + added[place] if place in added else rows
    one_h = in_order((first_h, got_h), masks, 0, width)
    one_l = in_order((first_l, got_l), masks, 0, width)
    two_h = in_order((first_h, got_h), masks, 1, width)
    two_l = in_order((first_l, got_l), masks, 1, width)
    gram = dot_t(one_h, two_h) + (dot_t(one_h, two_l) + dot_t(one_l, two_h))
    for i in range(k // m):
        row = 2 * k + i * k
        part = gram[:, i * m : (i + 1) * m]
        out_ref[row : row + k, :] = part if first else acc_ref[row : row + k, :] + part


def late(acc, got, firsts, zb, masks, base, first, k, width):
    m = zb.shape[1] // 2
    shapes = [jax.ShapeDtypeStruct((2 * k + k * k // m, m), F32)] + split_shapes(got)
    return pl.pallas_call(
        functools.partial(late_kernel, masks, width, base, k, first),
        out_shape=shapes,
        in_specs=vmem_specs(5),
        out_specs=vmem_specs(3),
        compiler_params=pltpu.CompilerParams(vmem_limit_bytes=LATE_VMEM),
    )(acc, got, *firsts, zb)


def apply_kernel(all_masks, width, bases, col_ref, total_ref, t_one_ref, t_two_ref, z_ref, *refs):
    halves, out_ref, true_ref, slot_ref = refs[:-3], refs[-3], refs[-2], refs[-1]
    k = t_one_ref.shape[0]
    m = z_ref.shape[1]
    blocks = k // width
    col = col_ref[0]

    def place(s):
        return pl.ds(pl.multiple_of(lax.bitwise_xor(col, s) * width, width), width)

    def solve(t_ref, coeff, row):
        for s in range(blocks):
            true_ref[place(s), :] = coeff[s * width : (s + 1) * width, :]
        true_ref[...] = exact(t_ref[...], true_ref[...])
        for s in range(blocks):
            slot_ref[row + s * width : row + (s + 1) * width, :] = true_ref[place(s), :]

    solve(t_two_ref, total_ref[k : 2 * k, :], k)
    coeff = total_ref[:k, :]
    for i in range(k // m):
        row = 2 * k + i * k
        coeff = coeff - exact(total_ref[row : row + k, :], slot_ref[k + i * m : k + (i + 1) * m, :])
    solve(t_one_ref, coeff, 0)
    x_h, x_l = split(slot_ref[...].T)
    x_both = jnp.concatenate([x_h, x_l], 0)
    for p, (base, masks) in enumerate(zip(bases, all_masks)):
        first_h, first_l, got_h, got_l = halves[4 * p : 4 * p + 4]
        n = first_h.shape[1]
        high = jnp.concatenate([in_order((first_h, got_h), masks, w, width) for w in range(2)], 0)
        low = jnp.concatenate([in_order((first_l, got_l), masks, w, width) for w in range(2)], 0)
        wide = dot(x_both, high)
        moved = wide[:m, :] + (wide[m:, :] + dot(x_h, low))
        out_ref[base : base + n, :] = z_ref[base : base + n, :] - moved.T


def apply(col, total, t_one, t_two, z, halves, all_masks, bases, width):
    k = t_one.shape[0]
    return pl.pallas_call(
        functools.partial(apply_kernel, all_masks, width, bases),
        out_shape=jax.ShapeDtypeStruct(z.shape, F32),
        in_specs=[pl.BlockSpec(memory_space=pltpu.SMEM)] + vmem_specs(4 + len(halves)),
        out_specs=pl.BlockSpec(memory_space=pltpu.VMEM),
        scratch_shapes=[pltpu.VMEM((k, z.shape[1]), F32), pltpu.VMEM((2 * k, z.shape[1]), F32)],
        compiler_params=pltpu.CompilerParams(vmem_limit_bytes=APPLY_VMEM),
    )(col, total, t_one, t_two, z, *halves)


def gather_pieces(own, size):
    n = own.shape[2]
    unit = n // sum(SHARES)
    cuts = [unit * sum(SHARES[:i]) for i in range(len(SHARES) + 1)]

    def widen(held, mask):
        data, masks = held
        got = swap(data, mask, size)
        return jnp.concatenate([data, got], 1), masks + [m ^ mask for m in masks]

    def part(held, low, high):
        return held[0][:, :, low:high], held[1]

    first = (own[:, :, : cuts[2]], [0])
    second = (own[:, :, cuts[2] :], [0])
    first, second = widen(first, XA), widen(second, YA)
    first, second = widen(first, XB), widen(second, YB)
    parts = [
        (part(first, 0, cuts[1]), YA, YB),
        (part(first, cuts[1], cuts[2]), YB, YA),
        (part(second, 0, cuts[3] - cuts[2]), XA, XB),
        (part(second, cuts[3] - cuts[2], cuts[4] - cuts[2]), XB, XA),
    ]
    parts = [(widen(held, near), last) for held, near, last in parts]
    pieces, masks = [], []
    for (data, held), last in parts:
        pieces.append((data, swap(data, last, size)))
        masks.append((held, [m ^ last for m in held]))
    return pieces, masks, cuts


def sum_over_row(part):
    r, m = part.shape
    group = PAIRS * NEAR
    rows = group * FAR
    pair = [(i, i ^ 1) for i in range(rows)]
    near = [[group * g + PAIRS * i + c for i in range(NEAR)] for g in range(FAR) for c in range(PAIRS)]
    far = [[i + group * g for g in range(FAR)] for i in range(group)]
    core = lax.axis_index("row") % PAIRS
    half = r // PAIRS
    kept = lax.dynamic_slice_in_dim(part, core * half, half, 0)
    given = lax.dynamic_slice_in_dim(part, (1 - core) * half, half, 0)
    mine = kept + lax.ppermute(given, "row", pair)
    blocks = lax.all_to_all(mine.reshape(NEAR, half // NEAR, m), "row", 0, 0, axis_index_groups=near, tiled=True)
    mine = jnp.sum(blocks, 0)
    blocks = lax.all_to_all(
        jnp.broadcast_to(mine[None], (FAR,) + mine.shape), "row", 0, 0, axis_index_groups=far, tiled=True
    )
    mine = jnp.sum(blocks, 0)
    blocks = lax.all_to_all(
        jnp.broadcast_to(mine[None], (NEAR,) + mine.shape), "row", 0, 0, axis_index_groups=near, tiled=True
    )
    mine = blocks.reshape(half, m)
    other = lax.ppermute(mine, "row", pair)
    return jnp.where(core == 0, jnp.concatenate([mine, other], 0), jnp.concatenate([other, mine], 0))


def body(size, z_slab, v_first, v_second, t_first, t_second):
    n, width = v_first.shape
    k = t_first.shape[0]
    own = lax.optimization_barrier(jnp.stack([v_first.T, v_second.T]))
    pieces, masks, cuts = gather_pieces(own, size)
    bases = cuts[:-1]
    part, z_both, firsts = early(z_slab, [piece[0] for piece in pieces], masks, bases, k, width)
    halves = []
    for p, base in enumerate(bases):
        part, *got = late(part, pieces[p][1], firsts[p], z_both, masks[p], base, p == 0, k, width)
        halves += [*firsts[p], *got]
    total = sum_over_row(part)
    col = lax.axis_index("col").astype(jnp.int32).reshape(1)
    return apply(col, total, t_first, t_second, z_slab, halves, masks, bases, width)


def solution(mesh):
    placed = (P("row", "col"), P("row", "col"), P("row", "col"), P(), P())
    return jax.shard_map(
        functools.partial(body, mesh.shape["col"]),
        mesh=mesh,
        in_specs=placed,
        out_specs=P("row", "col"),
        check_vma=False,
    )
```

```python
import functools

import jax
import jax.numpy as jnp
from jax import lax
from jax.experimental import pallas as pl
from jax.experimental.pallas import tpu as pltpu
from jax.sharding import PartitionSpec as P

F32 = jnp.float32
BF16 = jnp.bfloat16
LANES = 128
XA, XB, YA, YB = 1, 3, 4, 12
SHARES = (7, 5, 7, 5)
PAIRS = 2
NEAR = 4
FAR = 4
EARLY_VMEM = 24 << 20
LATE_VMEM = 16 << 20
APPLY_VMEM = 24 << 20


def dot(left, right):
    return jnp.dot(left, right, preferred_element_type=F32)


def dot_t(left, right):
    return lax.dot_general(left, right, (((1,), (1,)), ((), ())), preferred_element_type=F32)


def exact(left, right):
    return jnp.dot(left, right, precision=lax.Precision.HIGHEST, preferred_element_type=F32)


def split(x):
    high = x.astype(BF16)
    return high, (x - high.astype(F32)).astype(BF16)


def swap(x, mask, size):
    return lax.ppermute(x, "col", [(i, i ^ mask) for i in range(size)])


def in_order(pair, masks, row, width):
    blocks = {}
    for half, held in zip(pair, masks):
        for i, mask in enumerate(held):
            low = row * len(held) * width + i * width
            blocks[mask] = half[low : low + width, :]
    return jnp.concatenate([blocks[mask] for mask in sorted(blocks)], 0)


def scatter_rows(part, held, k, width):
    count = len(held)
    for which in range(2):
        for i, mask in enumerate(held):
            low = (which * count + i) * width
            yield which * k + mask * width, part[low : low + width, :]


def split_half(ref, high_ref, low_ref):
    rows = ref.shape[1]
    for which in range(2):
        high, low = split(ref[which])
        high_ref[which * rows : (which + 1) * rows, :] = high
        low_ref[which * rows : (which + 1) * rows, :] = low


def half_coeffs(high, low, z_both):
    m = z_both.shape[1] // 2
    wide = dot(high, z_both)
    return wide[:, :m] + (wide[:, m:] + dot(low, z_both[:, :m]))


def early_kernel(all_masks, width, bases, k, z_ref, *refs):
    count = len(bases)
    halves, acc_ref, zb_ref, out = refs[:count], refs[count], refs[count + 1], refs[count + 2 : 3 * count + 2]
    kept, sems = refs[3 * count + 2 : -1], refs[-1]
    m = z_ref.shape[1]
    copies = []
    acc_ref[...] = jnp.zeros_like(acc_ref)
    for p, base in enumerate(bases):
        n = halves[p].shape[2]
        z_h, z_l = split(z_ref[base : base + n, :])
        zb_ref[base : base + n, :m] = z_h
        zb_ref[base : base + n, m:] = z_l
        split_half(halves[p], out[2 * p], out[2 * p + 1])
        for i in (2 * p, 2 * p + 1):
            copies.append(pltpu.make_async_copy(out[i], kept[i], sems.at[i]))
            copies[-1].start()
        part = half_coeffs(out[2 * p][...], out[2 * p + 1][...], zb_ref[base : base + n, :])
        for place, rows in scatter_rows(part, all_masks[p][0], k, width):
            acc_ref[place : place + width, :] += rows
    for copy in copies:
        copy.wait()


def split_shapes(half):
    shape = jax.ShapeDtypeStruct((half.shape[0] * half.shape[1], half.shape[2]), BF16)
    return [shape, shape]


def vmem_specs(count):
    return [pl.BlockSpec(memory_space=pltpu.VMEM)] * count


def hbm_specs(count):
    return [pl.BlockSpec(memory_space=pltpu.HBM)] * count


def early(z, halves, all_masks, bases, k, width):
    n, m = z.shape
    shapes = [jax.ShapeDtypeStruct((2 * k, m), F32), jax.ShapeDtypeStruct((n, 2 * m), BF16)]
    split_halves = [shape for half in halves for shape in split_shapes(half)]
    count = len(split_halves)
    out = pl.pallas_call(
        functools.partial(early_kernel, all_masks, width, bases, k),
        out_shape=shapes + split_halves + split_halves,
        in_specs=vmem_specs(1 + len(halves)),
        out_specs=vmem_specs(2 + count) + hbm_specs(count),
        scratch_shapes=[pltpu.SemaphoreType.DMA((count,))],
        compiler_params=pltpu.CompilerParams(vmem_limit_bytes=EARLY_VMEM),
        cost_estimate=pl.CostEstimate(flops=6 * k * n * m, bytes_accessed=12 << 20, transcendentals=0),
    )(z, *halves)
    return out[0], out[1], out[2 : 2 + count], out[2 + count :]


def late_kernel(masks, width, base, k, first, acc_ref, got_ref, first_h, first_l, zb_ref, out_ref, *refs):
    kept, (got_h, got_l, sems) = refs[:2], refs[2:]
    n = got_ref.shape[2]
    m = zb_ref.shape[1] // 2
    split_half(got_ref, got_h, got_l)
    copies = [pltpu.make_async_copy(half, kept[i], sems.at[i]) for i, half in enumerate((got_h, got_l))]
    for copy in copies:
        copy.start()
    part = half_coeffs(got_h[...], got_l[...], zb_ref[base : base + n, :])
    added = {place: rows for place, rows in scatter_rows(part, masks[1], k, width)}
    for place in range(0, 2 * k, width):
        rows = acc_ref[place : place + width, :]
        out_ref[place : place + width, :] = rows + added[place] if place in added else rows
    one_h = in_order((first_h, got_h), masks, 0, width)
    one_l = in_order((first_l, got_l), masks, 0, width)
    two_h = in_order((first_h, got_h), masks, 1, width)
    two_l = in_order((first_l, got_l), masks, 1, width)
    gram = dot_t(one_h, two_h) + (dot_t(one_h, two_l) + dot_t(one_l, two_h))
    for i in range(k // m):
        row = 2 * k + i * k
        part = gram[:, i * m : (i + 1) * m]
        out_ref[row : row + k, :] = part if first else acc_ref[row : row + k, :] + part
    for copy in copies:
        copy.wait()


def late(acc, got, firsts, zb, masks, base, first, k, width):
    m = zb.shape[1] // 2
    split_got = split_shapes(got)
    return pl.pallas_call(
        functools.partial(late_kernel, masks, width, base, k, first),
        out_shape=[jax.ShapeDtypeStruct((2 * k + k * k // m, m), F32)] + split_got,
        in_specs=vmem_specs(5),
        out_specs=vmem_specs(1) + hbm_specs(2),
        scratch_shapes=[pltpu.VMEM(shape.shape, BF16) for shape in split_got] + [pltpu.SemaphoreType.DMA((2,))],
        compiler_params=pltpu.CompilerParams(vmem_limit_bytes=LATE_VMEM),
    )(acc, got, *firsts, zb)


def apply_kernel(all_masks, width, bases, place_ref, mine_ref, other_ref, t_one_ref, t_two_ref, z_ref, *refs):
    count = 4 * len(bases)
    halves, out_ref, held = refs[:count], refs[count], refs[count + 1 : 2 * count + 1]
    z_held, out_held, total_ref, true_ref, slot_ref, sems, z_sems, out_sems = refs[2 * count + 1 :]
    k = t_one_ref.shape[0]
    m = z_ref.shape[1]
    blocks = k // width
    ends = bases[1:] + [z_ref.shape[0]]
    loads = [pltpu.make_async_copy(half, held[i], sems.at[i]) for i, half in enumerate(halves)]
    z_loads = []
    for p, (base, end) in enumerate(zip(bases, ends)):
        rows = pl.ds(base, end - base)
        z_loads.append(pltpu.make_async_copy(z_ref.at[rows, :], z_held.at[rows, :], z_sems.at[p]))
    for p in range(len(bases)):
        for i in range(4 * p, 4 * p + 4):
            loads[i].start()
        z_loads[p].start()
    col, core = place_ref[0], place_ref[1]
    half = mine_ref.shape[0]
    total_ref[pl.ds(pl.multiple_of(core * half, half), half), :] = mine_ref[...]
    total_ref[pl.ds(pl.multiple_of((1 - core) * half, half), half), :] = other_ref[...]

    def place(s):
        return pl.ds(pl.multiple_of(lax.bitwise_xor(col, s) * width, width), width)

    def solve(t_ref, coeff, row):
        for s in range(blocks):
            true_ref[place(s), :] = coeff[s * width : (s + 1) * width, :]
        true_ref[...] = exact(t_ref[...], true_ref[...])
        for s in range(blocks):
            slot_ref[row + s * width : row + (s + 1) * width, :] = true_ref[place(s), :]

    solve(t_two_ref, total_ref[k : 2 * k, :], k)
    coeff = total_ref[:k, :]
    for i in range(k // m):
        row = 2 * k + i * k
        coeff = coeff - exact(total_ref[row : row + k, :], slot_ref[k + i * m : k + (i + 1) * m, :])
    solve(t_one_ref, coeff, 0)
    x_h, x_l = split(slot_ref[...].T)
    x_both = jnp.concatenate([x_h, x_l], 0)
    stores = []
    for p, (base, end, masks) in enumerate(zip(bases, ends, all_masks)):
        for load in loads[4 * p : 4 * p + 4] + [z_loads[p]]:
            load.wait()
        first_h, first_l, got_h, got_l = held[4 * p : 4 * p + 4]
        high = jnp.concatenate([in_order((first_h, got_h), masks, w, width) for w in range(2)], 0)
        low = jnp.concatenate([in_order((first_l, got_l), masks, w, width) for w in range(2)], 0)
        wide = dot(x_both, high)
        moved = wide[:m, :] + (wide[m:, :] + dot(x_h, low))
        out_held[base:end, :] = z_held[base:end, :] - moved.T
        rows = pl.ds(base, end - base)
        stores.append(pltpu.make_async_copy(out_held.at[rows, :], out_ref.at[rows, :], out_sems.at[p]))
        stores[-1].start()
    for store in stores:
        store.wait()


def apply(place, mine, other, t_one, t_two, z, halves, all_masks, bases, width):
    k, m = t_one.shape[0], z.shape[1]
    rows = pltpu.VMEM(z.shape, F32)
    dma = pltpu.SemaphoreType.DMA
    return pl.pallas_call(
        functools.partial(apply_kernel, all_masks, width, bases),
        out_shape=jax.ShapeDtypeStruct(z.shape, F32),
        in_specs=[pl.BlockSpec(memory_space=pltpu.SMEM)] + vmem_specs(4) + hbm_specs(1 + len(halves)),
        out_specs=pl.BlockSpec(memory_space=pltpu.HBM),
        scratch_shapes=[pltpu.VMEM(half.shape, BF16) for half in halves]
        + [rows, rows, pltpu.VMEM((2 * mine.shape[0], m), F32), pltpu.VMEM((k, m), F32), pltpu.VMEM((2 * k, m), F32)]
        + [dma((len(halves),)), dma((len(bases),)), dma((len(bases),))],
        compiler_params=pltpu.CompilerParams(vmem_limit_bytes=APPLY_VMEM),
    )(place, mine, other, t_one, t_two, z, *halves)


def gather_pieces(own, size):
    n = own.shape[2]
    unit = n // sum(SHARES)
    cuts = [unit * sum(SHARES[:i]) for i in range(len(SHARES) + 1)]

    def widen(held, mask):
        data, masks = held
        got = swap(data, mask, size)
        return jnp.concatenate([data, got], 1), masks + [m ^ mask for m in masks]

    def part(held, low, high):
        return held[0][:, :, low:high], held[1]

    first = (own[:, :, : cuts[2]], [0])
    second = (own[:, :, cuts[2] :], [0])
    first, second = widen(first, XA), widen(second, YA)
    first, second = widen(first, XB), widen(second, YB)
    parts = [
        (part(first, 0, cuts[1]), YA, YB),
        (part(first, cuts[1], cuts[2]), YB, YA),
        (part(second, 0, cuts[3] - cuts[2]), XA, XB),
        (part(second, cuts[3] - cuts[2], cuts[4] - cuts[2]), XB, XA),
    ]
    parts = [(widen(held, near), last) for held, near, last in parts]
    pieces, masks = [], []
    for (data, held), last in parts:
        pieces.append((data, swap(data, last, size)))
        masks.append((held, [m ^ last for m in held]))
    return pieces, masks, cuts


def sum_over_row(part):
    r, m = part.shape
    group = PAIRS * NEAR
    rows = group * FAR
    pair = [(i, i ^ 1) for i in range(rows)]
    near = [[group * g + PAIRS * i + c for i in range(NEAR)] for g in range(FAR) for c in range(PAIRS)]
    far = [[i + group * g for g in range(FAR)] for i in range(group)]
    core = lax.axis_index("row") % PAIRS
    half = r // PAIRS
    kept = lax.dynamic_slice_in_dim(part, core * half, half, 0)
    given = lax.dynamic_slice_in_dim(part, (1 - core) * half, half, 0)
    mine = kept + lax.ppermute(given, "row", pair)
    blocks = lax.all_to_all(mine.reshape(NEAR, half // NEAR, m), "row", 0, 0, axis_index_groups=near, tiled=True)
    mine = jnp.sum(blocks, 0)
    blocks = lax.all_to_all(
        jnp.broadcast_to(mine[None], (FAR,) + mine.shape), "row", 0, 0, axis_index_groups=far, tiled=True
    )
    mine = jnp.sum(blocks, 0)
    blocks = lax.all_to_all(
        jnp.broadcast_to(mine[None], (NEAR,) + mine.shape), "row", 0, 0, axis_index_groups=near, tiled=True
    )
    mine = blocks.reshape(half, m)
    return mine, lax.ppermute(mine, "row", pair), core


def body(size, z_slab, v_first, v_second, t_first, t_second):
    n, width = v_first.shape
    k = t_first.shape[0]
    own = lax.optimization_barrier(jnp.stack([v_first.T, v_second.T]))
    pieces, masks, cuts = gather_pieces(own, size)
    bases = cuts[:-1]
    part, z_both, firsts, kept = early(z_slab, [piece[0] for piece in pieces], masks, bases, k, width)
    halves = []
    for p, base in enumerate(bases):
        two = slice(2 * p, 2 * p + 2)
        part, *got = late(part, pieces[p][1], firsts[two], z_both, masks[p], base, p == 0, k, width)
        halves += [*kept[two], *got]
    mine, other, core = sum_over_row(part)
    place = jnp.stack([lax.axis_index("col"), core]).astype(jnp.int32)
    return apply(place, mine, other, t_first, t_second, z_slab, halves, masks, bases, width)


def solution(mesh):
    placed = (P("row", "col"), P("row", "col"), P("row", "col"), P(), P())
    return jax.shard_map(
        functools.partial(body, mesh.shape["col"]),
        mesh=mesh,
        in_specs=placed,
        out_specs=P("row", "col"),
        check_vma=False,
    )
```

```python
import functools

import jax
import jax.numpy as jnp
from jax import lax
from jax.experimental import pallas as pl
from jax.experimental.pallas import tpu as pltpu
from jax.sharding import PartitionSpec as P

F32 = jnp.float32
BF16 = jnp.bfloat16
LANES = 128
XA, XB, YA, YB = 1, 3, 4, 12
SHARES = (7, 5, 7, 5)
PAIRS = 2
NEAR = 4
FAR = 4
EARLY_VMEM = 24 << 20
LATE_VMEM = 16 << 20
APPLY_VMEM = 56 << 20


def dot(left, right):
    return jnp.dot(left, right, preferred_element_type=F32)


def dot_t(left, right):
    return lax.dot_general(left, right, (((1,), (1,)), ((), ())), preferred_element_type=F32)


def exact(left, right):
    return jnp.dot(left, right, precision=lax.Precision.HIGHEST, preferred_element_type=F32)


def split(x):
    high = x.astype(BF16)
    return high, (x - high.astype(F32)).astype(BF16)


def swap(x, mask, size):
    return lax.ppermute(x, "col", [(i, i ^ mask) for i in range(size)])


def in_order(pair, masks, row, width):
    blocks = {}
    for half, held in zip(pair, masks):
        for i, mask in enumerate(held):
            low = row * len(held) * width + i * width
            blocks[mask] = half[low : low + width, :]
    return jnp.concatenate([blocks[mask] for mask in sorted(blocks)], 0)


def scatter_rows(part, held, k, width):
    count = len(held)
    for which in range(2):
        for i, mask in enumerate(held):
            low = (which * count + i) * width
            yield which * k + mask * width, part[low : low + width, :]


def split_half(ref, high_ref, low_ref):
    rows = ref.shape[1]
    for which in range(2):
        high, low = split(ref[which])
        high_ref[which * rows : (which + 1) * rows, :] = high
        low_ref[which * rows : (which + 1) * rows, :] = low


def half_coeffs(high, low, z_both):
    m = z_both.shape[1] // 2
    wide = dot(high, z_both)
    return wide[:, :m] + (wide[:, m:] + dot(low, z_both[:, :m]))


def keep(half, kept, place, base, sem):
    rows, n = half.shape
    copy = pltpu.make_async_copy(half, kept.at[pl.ds(place * rows, rows), pl.ds(base, n)], sem)
    copy.start()
    return copy


def early_kernel(all_masks, width, bases, k, z_ref, *refs):
    count = len(bases)
    halves, acc_ref, zb_ref, out = refs[:count], refs[count], refs[count + 1], refs[count + 2 : 3 * count + 2]
    kept, sems = refs[3 * count + 2 :]
    m = z_ref.shape[1]
    copies = []
    acc_ref[...] = jnp.zeros_like(acc_ref)
    for p, base in enumerate(bases):
        n = halves[p].shape[2]
        z_h, z_l = split(z_ref[base : base + n, :])
        zb_ref[base : base + n, :m] = z_h
        zb_ref[base : base + n, m:] = z_l
        split_half(halves[p], out[2 * p], out[2 * p + 1])
        for i in range(2):
            copies.append(keep(out[2 * p + i], kept, 2 * i, base, sems.at[2 * p + i]))
        part = half_coeffs(out[2 * p][...], out[2 * p + 1][...], zb_ref[base : base + n, :])
        for place, rows in scatter_rows(part, all_masks[p][0], k, width):
            acc_ref[place : place + width, :] += rows
    for copy in copies:
        copy.wait()


def split_shapes(half):
    shape = jax.ShapeDtypeStruct((half.shape[0] * half.shape[1], half.shape[2]), BF16)
    return [shape, shape]


def vmem_specs(count):
    return [pl.BlockSpec(memory_space=pltpu.VMEM)] * count


def any_specs(count):
    return [pl.BlockSpec(memory_space=pl.ANY)] * count


def early(z, halves, all_masks, bases, k, width):
    n, m = z.shape
    shapes = [jax.ShapeDtypeStruct((2 * k, m), F32), jax.ShapeDtypeStruct((n, 2 * m), BF16)]
    split_halves = [shape for half in halves for shape in split_shapes(half)]
    count = len(split_halves)
    out = pl.pallas_call(
        functools.partial(early_kernel, all_masks, width, bases, k),
        out_shape=shapes + split_halves + [jax.ShapeDtypeStruct((4 * k, n), BF16)],
        in_specs=vmem_specs(1 + len(halves)),
        out_specs=vmem_specs(2 + count) + any_specs(1),
        scratch_shapes=[pltpu.SemaphoreType.DMA((count,))],
        compiler_params=pltpu.CompilerParams(vmem_limit_bytes=EARLY_VMEM),
        cost_estimate=pl.CostEstimate(flops=6 * k * n * m, bytes_accessed=12 << 20, transcendentals=0),
    )(z, *halves)
    return out[0], out[1], out[2 : 2 + count], out[2 + count]


def late_kernel(masks, width, base, k, first, acc_ref, got_ref, first_h, first_l, zb_ref, _, *refs):
    out_ref, kept, got_h, got_l, sems = refs
    n = got_ref.shape[2]
    m = zb_ref.shape[1] // 2
    split_half(got_ref, got_h, got_l)
    copies = [keep(half, kept, 2 * i + 1, base, sems.at[i]) for i, half in enumerate((got_h, got_l))]
    part = half_coeffs(got_h[...], got_l[...], zb_ref[base : base + n, :])
    added = {place: rows for place, rows in scatter_rows(part, masks[1], k, width)}
    for place in range(0, 2 * k, width):
        rows = acc_ref[place : place + width, :]
        out_ref[place : place + width, :] = rows + added[place] if place in added else rows
    one_h = in_order((first_h, got_h), masks, 0, width)
    one_l = in_order((first_l, got_l), masks, 0, width)
    two_h = in_order((first_h, got_h), masks, 1, width)
    two_l = in_order((first_l, got_l), masks, 1, width)
    gram = dot_t(one_h, two_h) + (dot_t(one_h, two_l) + dot_t(one_l, two_h))
    for i in range(k // m):
        row = 2 * k + i * k
        part = gram[:, i * m : (i + 1) * m]
        out_ref[row : row + k, :] = part if first else acc_ref[row : row + k, :] + part
    for copy in copies:
        copy.wait()


def late(acc, got, firsts, zb, kept, masks, base, first, k, width):
    m = zb.shape[1] // 2
    split_got = split_shapes(got)
    return pl.pallas_call(
        functools.partial(late_kernel, masks, width, base, k, first),
        out_shape=[jax.ShapeDtypeStruct((2 * k + k * k // m, m), F32), jax.ShapeDtypeStruct(kept.shape, BF16)],
        in_specs=vmem_specs(5) + any_specs(1),
        out_specs=vmem_specs(1) + any_specs(1),
        input_output_aliases={5: 1},
        scratch_shapes=[pltpu.VMEM(shape.shape, BF16) for shape in split_got] + [pltpu.SemaphoreType.DMA((2,))],
        compiler_params=pltpu.CompilerParams(vmem_limit_bytes=LATE_VMEM),
    )(acc, got, *firsts, zb, kept)


def apply_kernel(all_masks, width, bases, place_ref, mine_ref, other_ref, t_one_ref, t_two_ref, z_ref, kept_ref, *refs):
    out_ref, held, z_held, out_held, total_ref, true_ref, slot_ref, sems, z_sems, out_sems = refs
    k = t_one_ref.shape[0]
    m = z_ref.shape[1]
    blocks = k // width
    ends = bases[1:] + [z_ref.shape[0]]
    loads, z_loads = [], []
    for p, (base, end) in enumerate(zip(bases, ends)):
        rows, lanes = pl.ds(base, end - base), (slice(None), pl.ds(base, end - base))
        loads.append(pltpu.make_async_copy(kept_ref.at[lanes], held.at[lanes], sems.at[p]))
        z_loads.append(pltpu.make_async_copy(z_ref.at[rows, :], z_held.at[rows, :], z_sems.at[p]))
        loads[p].start()
        z_loads[p].start()
    col, core = place_ref[0], place_ref[1]
    half = mine_ref.shape[0]
    total_ref[pl.ds(pl.multiple_of(core * half, half), half), :] = mine_ref[...]
    total_ref[pl.ds(pl.multiple_of((1 - core) * half, half), half), :] = other_ref[...]

    def place(s):
        return pl.ds(pl.multiple_of(lax.bitwise_xor(col, s) * width, width), width)

    def solve(t_ref, coeff, row):
        for s in range(blocks):
            true_ref[place(s), :] = coeff[s * width : (s + 1) * width, :]
        true_ref[...] = exact(t_ref[...], true_ref[...])
        for s in range(blocks):
            slot_ref[row + s * width : row + (s + 1) * width, :] = true_ref[place(s), :]

    solve(t_two_ref, total_ref[k : 2 * k, :], k)
    coeff = total_ref[:k, :]
    for i in range(k // m):
        row = 2 * k + i * k
        coeff = coeff - exact(total_ref[row : row + k, :], slot_ref[k + i * m : k + (i + 1) * m, :])
    solve(t_one_ref, coeff, 0)
    x_h, x_l = split(slot_ref[...].T)
    x_both = jnp.concatenate([x_h, x_l], 0)
    stores = []
    for p, (base, end, masks) in enumerate(zip(bases, ends, all_masks)):
        loads[p].wait()
        z_loads[p].wait()
        first_h, got_h, first_l, got_l = [held.at[pl.ds(i * k, k), pl.ds(base, end - base)] for i in range(4)]
        high = jnp.concatenate([in_order((first_h, got_h), masks, w, width) for w in range(2)], 0)
        low = jnp.concatenate([in_order((first_l, got_l), masks, w, width) for w in range(2)], 0)
        wide = dot(x_both, high)
        moved = wide[:m, :] + (wide[m:, :] + dot(x_h, low))
        out_held[base:end, :] = z_held[base:end, :] - moved.T
        rows = pl.ds(base, end - base)
        stores.append(pltpu.make_async_copy(out_held.at[rows, :], out_ref.at[rows, :], out_sems.at[p]))
        stores[-1].start()
    for store in stores:
        store.wait()


def apply(place, mine, other, t_one, t_two, z, kept, all_masks, bases, width):
    k, m = t_one.shape[0], z.shape[1]
    rows = pltpu.VMEM(z.shape, F32)
    dma = pltpu.SemaphoreType.DMA
    return pl.pallas_call(
        functools.partial(apply_kernel, all_masks, width, bases),
        out_shape=jax.ShapeDtypeStruct(z.shape, F32),
        in_specs=[pl.BlockSpec(memory_space=pltpu.SMEM)] + vmem_specs(4) + any_specs(2),
        out_specs=pl.BlockSpec(memory_space=pl.ANY),
        scratch_shapes=[pltpu.VMEM(kept.shape, BF16), rows, rows, pltpu.VMEM((2 * mine.shape[0], m), F32), pltpu.VMEM((k, m), F32), pltpu.VMEM((2 * k, m), F32)]
        + [dma((len(bases),))] * 3,
        compiler_params=pltpu.CompilerParams(vmem_limit_bytes=APPLY_VMEM),
    )(place, mine, other, t_one, t_two, z, kept)


def gather_pieces(own, size):
    n = own.shape[2]
    unit = n // sum(SHARES)
    cuts = [unit * sum(SHARES[:i]) for i in range(len(SHARES) + 1)]

    def widen(held, mask):
        data, masks = held
        got = swap(data, mask, size)
        return jnp.concatenate([data, got], 1), masks + [m ^ mask for m in masks]

    def part(held, low, high):
        return held[0][:, :, low:high], held[1]

    first = (own[:, :, : cuts[2]], [0])
    second = (own[:, :, cuts[2] :], [0])
    first, second = widen(first, XA), widen(second, YA)
    first, second = widen(first, XB), widen(second, YB)
    parts = [
        (part(first, 0, cuts[1]), YA, YB),
        (part(first, cuts[1], cuts[2]), YB, YA),
        (part(second, 0, cuts[3] - cuts[2]), XA, XB),
        (part(second, cuts[3] - cuts[2], cuts[4] - cuts[2]), XB, XA),
    ]
    parts = [(widen(held, near), last) for held, near, last in parts]
    pieces, masks = [], []
    for (data, held), last in parts:
        pieces.append((data, swap(data, last, size)))
        masks.append((held, [m ^ last for m in held]))
    return pieces, masks, cuts


def sum_over_row(part):
    r, m = part.shape
    group = PAIRS * NEAR
    rows = group * FAR
    pair = [(i, i ^ 1) for i in range(rows)]
    near = [[group * g + PAIRS * i + c for i in range(NEAR)] for g in range(FAR) for c in range(PAIRS)]
    far = [[i + group * g for g in range(FAR)] for i in range(group)]
    core = lax.axis_index("row") % PAIRS
    half = r // PAIRS
    kept = lax.dynamic_slice_in_dim(part, core * half, half, 0)
    given = lax.dynamic_slice_in_dim(part, (1 - core) * half, half, 0)
    mine = kept + lax.ppermute(given, "row", pair)
    blocks = lax.all_to_all(mine.reshape(NEAR, half // NEAR, m), "row", 0, 0, axis_index_groups=near, tiled=True)
    mine = jnp.sum(blocks, 0)
    blocks = lax.all_to_all(
        jnp.broadcast_to(mine[None], (FAR,) + mine.shape), "row", 0, 0, axis_index_groups=far, tiled=True
    )
    mine = jnp.sum(blocks, 0)
    blocks = lax.all_to_all(
        jnp.broadcast_to(mine[None], (NEAR,) + mine.shape), "row", 0, 0, axis_index_groups=near, tiled=True
    )
    mine = blocks.reshape(half, m)
    return mine, lax.ppermute(mine, "row", pair), core


def body(size, z_slab, v_first, v_second, t_first, t_second):
    n, width = v_first.shape
    k = t_first.shape[0]
    own = lax.optimization_barrier(jnp.stack([v_first.T, v_second.T]))
    pieces, masks, cuts = gather_pieces(own, size)
    bases = cuts[:-1]
    part, z_both, firsts, kept = early(z_slab, [piece[0] for piece in pieces], masks, bases, k, width)
    for p, base in enumerate(bases):
        two = slice(2 * p, 2 * p + 2)
        part, kept = late(part, pieces[p][1], firsts[two], z_both, kept, masks[p], base, p == 0, k, width)
    mine, other, core = sum_over_row(part)
    place = jnp.stack([lax.axis_index("col"), core]).astype(jnp.int32)
    return apply(place, mine, other, t_first, t_second, z_slab, kept, masks, bases, width)


def solution(mesh):
    placed = (P("row", "col"), P("row", "col"), P("row", "col"), P(), P())
    return jax.shard_map(
        functools.partial(body, mesh.shape["col"]),
        mesh=mesh,
        in_specs=placed,
        out_specs=P("row", "col"),
        check_vma=False,
    )
```

```python
import functools

import jax
import jax.numpy as jnp
from jax import lax
from jax.experimental import pallas as pl
from jax.experimental.pallas import tpu as pltpu
from jax.sharding import PartitionSpec as P

F32 = jnp.float32
BF16 = jnp.bfloat16
NEXT, BACK = 1, 3
SIDE = 4
SHARES = (7, 5, 7, 5)
PAIRS = 2
NEAR = 4
FAR = 4
GRANT = 32 << 20
PLANES = 6


def dot(left, right):
    return jnp.dot(left, right, preferred_element_type=F32)


def dot_t(left, right):
    return lax.dot_general(left, right, (((1,), (1,)), ((), ())), preferred_element_type=F32)


def exact(left, right):
    return jnp.dot(left, right, precision=lax.Precision.HIGHEST, preferred_element_type=F32)


def split(x):
    high = x.astype(BF16)
    return high, (x - high.astype(F32)).astype(BF16)


class Piece:
    def __init__(self, base, size, x_first, steps):
        self.base, self.size, self.x_first, self.steps = base, size, x_first, steps
        self.masks = [0, steps[0], steps[1], steps[0] ^ steps[1]]

    def chunk(self, place_ref, pos):
        y, x = place_ref[0], place_ref[1]
        mask, other = self.masks[pos // SIDE], pos % SIDE
        if self.x_first:
            return lax.bitwise_xor(y, mask) * SIDE + other
        return other * SIDE + lax.bitwise_xor(x, mask)


def block(place, width, base=0):
    return pl.ds(pl.multiple_of(base + place * width, width), width)


def half_coeffs(high, low, z_both):
    m = z_both.shape[1] // 2
    wide = dot(high, z_both)
    return wide[:, :m] + (wide[:, m:] + dot(low, z_both[:, :m]))


def add_coeffs(out_ref, part, place_ref, piece, first, k, width):
    for i in range(part.shape[0] // (2 * width)):
        chunk = piece.chunk(place_ref, first + i)
        for which in range(2):
            low = (2 * i + which) * width
            out_ref[block(chunk, width, which * k), :] += part[low : low + width, :]


def keep(half, kept, row, base, sem):
    rows, n = half.shape
    copy = pltpu.make_async_copy(half, kept.at[0, pl.ds(row, rows), pl.ds(base, n)], sem)
    copy.start()
    return copy


def early_kernel(pieces, k, width, place_ref, z_ref, *refs):
    count = len(pieces)
    halves, acc_ref, zb_ref, out = refs[:count], refs[count], refs[count + 1], refs[count + 2 : 3 * count + 2]
    kept, sems = refs[3 * count + 2 :]
    m = z_ref.shape[1]
    acc_ref[...] = jnp.zeros_like(acc_ref)
    copies = []
    for p, piece in enumerate(pieces):
        rows = slice(piece.base, piece.base + piece.size)
        zb_ref[rows, :m], zb_ref[rows, m:] = split(z_ref[rows, :])
        out[2 * p][...], out[2 * p + 1][...] = split(halves[p][...])
        for i in range(2):
            copies.append(keep(out[2 * p + i], kept, 2 * i * k, piece.base, sems.at[2 * p + i]))
        part = half_coeffs(out[2 * p][...], out[2 * p + 1][...], zb_ref[rows, :])
        add_coeffs(acc_ref, part, place_ref, piece, 0, k, width)
    for copy in copies:
        copy.wait()


def vmem_specs(count):
    return [pl.BlockSpec(memory_space=pltpu.VMEM)] * count


def any_specs(count):
    return [pl.BlockSpec(memory_space=pl.ANY)] * count


SMEM = [pl.BlockSpec(memory_space=pltpu.SMEM)]


def early(place, z, halves, pieces, k, width):
    n, m = z.shape
    pairs = [jax.ShapeDtypeStruct(half.shape, BF16) for half in halves for _ in range(2)]
    shapes = [jax.ShapeDtypeStruct((2 * k, m), F32), jax.ShapeDtypeStruct((n, 2 * m), BF16)] + pairs
    out = pl.pallas_call(
        functools.partial(early_kernel, pieces, k, width),
        out_shape=shapes + [jax.ShapeDtypeStruct((PLANES, 4 * k, n), BF16)],
        in_specs=SMEM + vmem_specs(1 + len(halves)),
        out_specs=vmem_specs(len(shapes)) + any_specs(1),
        scratch_shapes=[pltpu.SemaphoreType.DMA((len(pairs),))],
        compiler_params=pltpu.CompilerParams(vmem_limit_bytes=GRANT),
        cost_estimate=pl.CostEstimate(flops=6 * k * n * m, bytes_accessed=12 << 20, transcendentals=0),
    )(place, z, *halves)
    return out[0], out[1], out[2:-1], out[-1]


def late_kernel(piece, first, k, width, place_ref, acc_ref, got_ref, first_h, first_l, zb_ref, _, *refs):
    out_ref, kept, got_h, got_l, two_h, two_l, sems = refs
    m = zb_ref.shape[1] // 2
    got_h[...], got_l[...] = split(got_ref[...])
    copies = [keep(half, kept, (2 * i + 1) * k, piece.base, sems.at[i]) for i, half in enumerate((got_h, got_l))]
    half = k // (2 * width)
    chunks = [piece.chunk(place_ref, pos) for pos in range(2 * half)]
    one = []
    for own, got, two in ((first_h, got_h, two_h), (first_l, got_l, two_l)):
        blocks = []
        for pos, chunk in enumerate(chunks):
            ref, low = (own, got)[pos // half], pos % half * 2 * width
            blocks.append(ref[low : low + width, :])
            two[block(chunk, width), :] = ref[low + width : low + 2 * width, :]
        one.append(jnp.concatenate(blocks, 0))
    out_ref[: 2 * k, :] = acc_ref[: 2 * k, :]
    part = half_coeffs(got_h[...], got_l[...], zb_ref[piece.base : piece.base + piece.size, :])
    add_coeffs(out_ref, part, place_ref, piece, half, k, width)
    high = two_h[...]
    gram = dot_t(one[0], high) + (dot_t(one[0], two_l[...]) + dot_t(one[1], high))
    for pos, chunk in enumerate(chunks):
        for i in range(k // m):
            part = gram[pos * width : (pos + 1) * width, i * m : (i + 1) * m]
            rows = block(chunk, width, (2 + i) * k)
            out_ref[rows, :] = part if first else acc_ref[rows, :] + part
    for copy in copies:
        copy.wait()


def late(place, acc, got, firsts, zb, kept, piece, first, k, width):
    m = zb.shape[1] // 2
    rows = pltpu.VMEM(got.shape, BF16)
    return pl.pallas_call(
        functools.partial(late_kernel, piece, first, k, width),
        out_shape=[jax.ShapeDtypeStruct((2 * k + k * k // m, m), F32), jax.ShapeDtypeStruct(kept.shape, BF16)],
        in_specs=SMEM + vmem_specs(5) + any_specs(1),
        out_specs=vmem_specs(1) + any_specs(1),
        input_output_aliases={6: 1},
        scratch_shapes=[rows] * 4 + [pltpu.SemaphoreType.DMA((2,))],
        compiler_params=pltpu.CompilerParams(vmem_limit_bytes=GRANT),
    )(place, acc, got, *firsts, zb, kept)


def apply_kernel(pieces, width, place_ref, mine_ref, other_ref, t_one_ref, t_two_ref, z_ref, kept_ref, *refs):
    out_ref, held, z_held, out_held, total_ref, x_ref, slot_ref, sems, z_sems, out_sems = refs
    k = t_one_ref.shape[0]
    m = z_ref.shape[1]
    loads, z_loads = [], []
    for p, piece in enumerate(pieces):
        lanes = pl.ds(piece.base, piece.size)
        loads.append(pltpu.make_async_copy(kept_ref.at[0, :, lanes], held.at[:, lanes], sems.at[p]))
        z_loads.append(pltpu.make_async_copy(z_ref.at[lanes, :], z_held.at[lanes, :], z_sems.at[p]))
        loads[p].start()
        z_loads[p].start()
    core = place_ref[2]
    half = mine_ref.shape[0]
    total_ref[block(core, half), :] = mine_ref[...]
    total_ref[block(1 - core, half), :] = other_ref[...]
    x_ref[k:, :] = exact(t_two_ref[...], total_ref[k : 2 * k, :])
    coeff = total_ref[:k, :]
    for i in range(k // m):
        row = (2 + i) * k
        coeff = coeff - exact(total_ref[row : row + k, :], x_ref[k + i * m : k + (i + 1) * m, :])
    x_ref[:k, :] = exact(t_one_ref[...], coeff)
    stores = []
    for p, piece in enumerate(pieces):
        for pos in range(k // width):
            chunk = piece.chunk(place_ref, pos)
            for which in range(2):
                low = (2 * pos + which) * width
                slot_ref[low : low + width, :] = x_ref[block(chunk, width, which * k), :]
        x_h, x_l = split(slot_ref[...].T)
        x_both = jnp.concatenate([x_h, x_l], 0)
        loads[p].wait()
        z_loads[p].wait()
        rows = slice(piece.base, piece.base + piece.size)
        wide = dot(x_both, held[: 2 * k, rows])
        moved = wide[:m, :] + (wide[m:, :] + dot(x_h, held[2 * k :, rows]))
        out_held[rows, :] = z_held[rows, :] - moved.T
        lanes = pl.ds(piece.base, piece.size)
        stores.append(pltpu.make_async_copy(out_held.at[lanes, :], out_ref.at[lanes, :], out_sems.at[p]))
        stores[-1].start()
    for store in stores:
        store.wait()


def apply(place, mine, other, t_one, t_two, z, kept, pieces, width):
    k, m = t_one.shape[0], z.shape[1]
    rows = pltpu.VMEM(z.shape, F32)
    coeffs = pltpu.VMEM((2 * k, m), F32)
    return pl.pallas_call(
        functools.partial(apply_kernel, pieces, width),
        out_shape=jax.ShapeDtypeStruct(z.shape, F32),
        in_specs=SMEM + vmem_specs(4) + any_specs(2),
        out_specs=pl.BlockSpec(memory_space=pl.ANY),
        scratch_shapes=[pltpu.VMEM(kept.shape[1:], BF16), rows, rows, pltpu.VMEM((2 * mine.shape[0], m), F32)]
        + [coeffs, coeffs]
        + [pltpu.SemaphoreType.DMA((len(pieces),))] * 3,
        compiler_params=pltpu.CompilerParams(vmem_limit_bytes=GRANT),
    )(place, mine, other, t_one, t_two, z, kept)


def line(along_x):
    if along_x:
        return [[SIDE * y + x for x in range(SIDE)] for y in range(SIDE)]
    return [[SIDE * y + x for y in range(SIDE)] for x in range(SIDE)]


def gather_line(data, along_x):
    spread = jnp.broadcast_to(data[None], (SIDE,) + data.shape)
    got = lax.all_to_all(spread, "col", 0, 0, axis_index_groups=line(along_x), tiled=True)
    return got.reshape(SIDE * data.shape[0], data.shape[1])


def swap(data, mask, along_x):
    mask = mask if along_x else SIDE * mask
    return lax.ppermute(data, "col", [(i, i ^ mask) for i in range(SIDE * SIDE)])


def gather_pieces(own):
    unit = own.shape[1] // sum(SHARES)
    sizes = [unit * share for share in SHARES]
    pieces, halves = [], []
    for pair, x_first in ((0, True), (2, False)):
        base = sum(sizes[:pair])
        whole = gather_line(own[:, base : base + sizes[pair] + sizes[pair + 1]], x_first)
        for i, steps in ((0, (NEXT, BACK)), (1, (BACK, NEXT))):
            low = i * sizes[pair]
            piece = Piece(base + low, sizes[pair + i], x_first, steps)
            data = whole[:, low : low + piece.size]
            data = jnp.concatenate([data, swap(data, steps[0], not x_first)], 0)
            pieces.append(piece)
            halves.append((data, swap(data, steps[1], not x_first)))
    return pieces, halves


def sum_over_row(part):
    r, m = part.shape
    group = PAIRS * NEAR
    rows = group * FAR
    pair = [(i, i ^ 1) for i in range(rows)]
    near = [[group * g + PAIRS * i + c for i in range(NEAR)] for g in range(FAR) for c in range(PAIRS)]
    far = [[i + group * g for g in range(FAR)] for i in range(group)]
    core = lax.axis_index("row") % PAIRS
    half = r // PAIRS
    kept = lax.dynamic_slice_in_dim(part, core * half, half, 0)
    given = lax.dynamic_slice_in_dim(part, (1 - core) * half, half, 0)
    mine = kept + lax.ppermute(given, "row", pair)
    blocks = lax.all_to_all(mine.reshape(NEAR, half // NEAR, m), "row", 0, 0, axis_index_groups=near, tiled=True)
    mine = jnp.sum(blocks, 0)
    blocks = lax.all_to_all(
        jnp.broadcast_to(mine[None], (FAR,) + mine.shape), "row", 0, 0, axis_index_groups=far, tiled=True
    )
    mine = jnp.sum(blocks, 0)
    blocks = lax.all_to_all(
        jnp.broadcast_to(mine[None], (NEAR,) + mine.shape), "row", 0, 0, axis_index_groups=near, tiled=True
    )
    mine = blocks.reshape(half, m)
    return mine, lax.ppermute(mine, "row", pair)


def body(z_slab, v_first, v_second, t_first, t_second):
    width = v_first.shape[1]
    k = t_first.shape[0]
    own = lax.optimization_barrier(jnp.concatenate([v_first.T, v_second.T], 0))
    pieces, halves = gather_pieces(own)
    col, row = lax.axis_index("col"), lax.axis_index("row")
    place = lax.optimization_barrier(jnp.stack([col // SIDE, col % SIDE, row % PAIRS]).astype(jnp.int32))
    part, z_both, firsts, kept = early(place, z_slab, [half[0] for half in halves], pieces, k, width)
    for p, piece in enumerate(pieces):
        two = firsts[2 * p : 2 * p + 2]
        part, kept = late(place, part, halves[p][1], two, z_both, kept, piece, p == 0, k, width)
    mine, other = sum_over_row(part)
    return apply(place, mine, other, t_first, t_second, z_slab, kept, pieces, width)


def solution(mesh):
    placed = (P("row", "col"), P("row", "col"), P("row", "col"), P(), P())
    return jax.shard_map(
        body,
        mesh=mesh,
        in_specs=placed,
        out_specs=P("row", "col"),
        check_vma=False,
    )
```

```python
import functools

import jax
import jax.numpy as jnp
from jax import lax
from jax.experimental import pallas as pl
from jax.experimental.pallas import tpu as pltpu
from jax.sharding import PartitionSpec as P

F32 = jnp.float32
BF16 = jnp.bfloat16
XA, XB, YA, YB = 1, 3, 4, 12
SHARES = (7, 5, 7, 5)
PAIRS = 2
NEAR = 4
FAR = 4
GRANT = 32 << 20
PLANES = 6


def dot(left, right):
    return jnp.dot(left, right, preferred_element_type=F32)


def dot_t(left, right):
    return lax.dot_general(left, right, (((1,), (1,)), ((), ())), preferred_element_type=F32)


def exact(left, right):
    return jnp.dot(left, right, precision=lax.Precision.HIGHEST, preferred_element_type=F32)


def split(x):
    high = x.astype(BF16)
    return high, (x - high.astype(F32)).astype(BF16)


class Piece:
    def __init__(self, base, size, masks):
        self.base, self.size, self.masks = base, size, masks


def block(place, width, base=0):
    return pl.ds(pl.multiple_of(base + place * width, width), width)


def half_coeffs(high, low, z_both):
    m = z_both.shape[1] // 2
    wide = dot(high, z_both)
    return wide[:, :m] + (wide[:, m:] + dot(low, z_both[:, :m]))


def add_coeffs(out_ref, part, masks, k, width):
    for i, mask in enumerate(masks):
        for which in range(2):
            low, place = (2 * i + which) * width, which * k + mask * width
            out_ref[place : place + width, :] += part[low : low + width, :]


def keep(half, kept, row, base, sem):
    rows, n = half.shape
    copy = pltpu.make_async_copy(half, kept.at[0, pl.ds(row, rows), pl.ds(base, n)], sem)
    copy.start()
    return copy


def early_kernel(pieces, k, width, z_ref, *refs):
    count = len(pieces)
    halves, acc_ref, zb_ref, out = refs[:count], refs[count], refs[count + 1], refs[count + 2 : 3 * count + 2]
    kept, sems = refs[3 * count + 2 :]
    m = z_ref.shape[1]
    acc_ref[...] = jnp.zeros_like(acc_ref)
    copies = []
    for p, piece in enumerate(pieces):
        rows = slice(piece.base, piece.base + piece.size)
        zb_ref[rows, :m], zb_ref[rows, m:] = split(z_ref[rows, :])
        out[2 * p][...], out[2 * p + 1][...] = split(halves[p][...])
        for i in range(2):
            copies.append(keep(out[2 * p + i], kept, 2 * i * k, piece.base, sems.at[2 * p + i]))
        part = half_coeffs(out[2 * p][...], out[2 * p + 1][...], zb_ref[rows, :])
        add_coeffs(acc_ref, part, piece.masks[: len(piece.masks) // 2], k, width)
    for copy in copies:
        copy.wait()


def vmem_specs(count):
    return [pl.BlockSpec(memory_space=pltpu.VMEM)] * count


def any_specs(count):
    return [pl.BlockSpec(memory_space=pl.ANY)] * count


SMEM = [pl.BlockSpec(memory_space=pltpu.SMEM)]


def early(z, halves, pieces, k, width):
    n, m = z.shape
    pairs = [jax.ShapeDtypeStruct(half.shape, BF16) for half in halves for _ in range(2)]
    shapes = [jax.ShapeDtypeStruct((2 * k, m), F32), jax.ShapeDtypeStruct((n, 2 * m), BF16)] + pairs
    out = pl.pallas_call(
        functools.partial(early_kernel, pieces, k, width),
        out_shape=shapes + [jax.ShapeDtypeStruct((PLANES, 4 * k, n), BF16)],
        in_specs=vmem_specs(1 + len(halves)),
        out_specs=vmem_specs(len(shapes)) + any_specs(1),
        scratch_shapes=[pltpu.SemaphoreType.DMA((len(pairs),))],
        compiler_params=pltpu.CompilerParams(vmem_limit_bytes=GRANT),
        cost_estimate=pl.CostEstimate(flops=6 * k * n * m, bytes_accessed=12 << 20, transcendentals=0),
    )(z, *halves)
    return out[0], out[1], out[2:-1], out[-1]


def late_kernel(piece, first, k, width, acc_ref, got_ref, first_h, first_l, zb_ref, _, *refs):
    out_ref, kept, got_h, got_l, sems = refs
    m = zb_ref.shape[1] // 2
    got_h[...], got_l[...] = split(got_ref[...])
    copies = [keep(half, kept, (2 * i + 1) * k, piece.base, sems.at[i]) for i, half in enumerate((got_h, got_l))]
    half = k // (2 * width)

    def panel(which, own, got):
        blocks = [None] * (2 * half)
        for pos, mask in enumerate(piece.masks):
            ref, low = (own, got)[pos // half], (pos % half * 2 + which) * width
            blocks[mask] = ref[low : low + width, :]
        return jnp.concatenate(blocks, 0)

    out_ref[: 2 * k, :] = acc_ref[: 2 * k, :]
    part = half_coeffs(got_h[...], got_l[...], zb_ref[piece.base : piece.base + piece.size, :])
    add_coeffs(out_ref, part, piece.masks[half:], k, width)
    one_h, one_l, two_h, two_l = [panel(i, *pair) for i in range(2) for pair in ((first_h, got_h), (first_l, got_l))]
    gram = dot_t(one_h, two_h) + (dot_t(one_h, two_l) + dot_t(one_l, two_h))
    for i in range(k // m):
        rows, part = slice((2 + i) * k, (3 + i) * k), gram[:, i * m : (i + 1) * m]
        out_ref[rows, :] = part if first else acc_ref[rows, :] + part
    for copy in copies:
        copy.wait()


def late(acc, got, firsts, zb, kept, piece, first, k, width):
    m = zb.shape[1] // 2
    rows = pltpu.VMEM(got.shape, BF16)
    return pl.pallas_call(
        functools.partial(late_kernel, piece, first, k, width),
        out_shape=[jax.ShapeDtypeStruct((2 * k + k * k // m, m), F32), jax.ShapeDtypeStruct(kept.shape, BF16)],
        in_specs=vmem_specs(5) + any_specs(1),
        out_specs=vmem_specs(1) + any_specs(1),
        input_output_aliases={5: 1},
        scratch_shapes=[rows] * 2 + [pltpu.SemaphoreType.DMA((2,))],
        compiler_params=pltpu.CompilerParams(vmem_limit_bytes=GRANT),
    )(acc, got, *firsts, zb, kept)


def apply_kernel(pieces, width, place_ref, mine_ref, other_ref, t_one_ref, t_two_ref, z_ref, kept_ref, *refs):
    out_ref, held, z_held, out_held, total_ref, x_ref, slot_ref, sems, z_sems, out_sems = refs
    k = t_one_ref.shape[0]
    m = z_ref.shape[1]
    loads, z_loads = [], []
    for p, piece in enumerate(pieces):
        lanes = pl.ds(piece.base, piece.size)
        loads.append(pltpu.make_async_copy(kept_ref.at[0, :, lanes], held.at[:, lanes], sems.at[p]))
        z_loads.append(pltpu.make_async_copy(z_ref.at[lanes, :], z_held.at[lanes, :], z_sems.at[p]))
        loads[p].start()
        z_loads[p].start()
    core = place_ref[1]
    half = mine_ref.shape[0]
    total_ref[block(core, half), :] = mine_ref[...]
    total_ref[block(1 - core, half), :] = other_ref[...]
    col = place_ref[0]

    def solve(t_ref, coeff, row):
        for mask in range(k // width):
            slot_ref[block(lax.bitwise_xor(col, mask), width), :] = coeff[mask * width : (mask + 1) * width, :]
        slot_ref[:k, :] = exact(t_ref[...], slot_ref[:k, :])
        for mask in range(k // width):
            x_ref[row + mask * width : row + (mask + 1) * width, :] = slot_ref[block(lax.bitwise_xor(col, mask), width), :]

    solve(t_two_ref, total_ref[k : 2 * k, :], k)
    coeff = total_ref[:k, :]
    for i in range(k // m):
        row = (2 + i) * k
        coeff = coeff - exact(total_ref[row : row + k, :], x_ref[k + i * m : k + (i + 1) * m, :])
    solve(t_one_ref, coeff, 0)
    stores = []
    for p, piece in enumerate(pieces):
        for pos, mask in enumerate(piece.masks):
            for which in range(2):
                low, row = (2 * pos + which) * width, which * k + mask * width
                slot_ref[low : low + width, :] = x_ref[row : row + width, :]
        x_h, x_l = split(slot_ref[...].T)
        x_both = jnp.concatenate([x_h, x_l], 0)
        loads[p].wait()
        z_loads[p].wait()
        rows = slice(piece.base, piece.base + piece.size)
        wide = dot(x_both, held[: 2 * k, rows])
        moved = wide[:m, :] + (wide[m:, :] + dot(x_h, held[2 * k :, rows]))
        out_held[rows, :] = z_held[rows, :] - moved.T
        lanes = pl.ds(piece.base, piece.size)
        stores.append(pltpu.make_async_copy(out_held.at[lanes, :], out_ref.at[lanes, :], out_sems.at[p]))
        stores[-1].start()
    for store in stores:
        store.wait()


def apply(place, mine, other, t_one, t_two, z, kept, pieces, width):
    k, m = t_one.shape[0], z.shape[1]
    rows = pltpu.VMEM(z.shape, F32)
    coeffs = pltpu.VMEM((2 * k, m), F32)
    return pl.pallas_call(
        functools.partial(apply_kernel, pieces, width),
        out_shape=jax.ShapeDtypeStruct(z.shape, F32),
        in_specs=SMEM + vmem_specs(4) + any_specs(2),
        out_specs=pl.BlockSpec(memory_space=pl.ANY),
        scratch_shapes=[pltpu.VMEM(kept.shape[1:], BF16), rows, rows, pltpu.VMEM((2 * mine.shape[0], m), F32)]
        + [coeffs, coeffs]
        + [pltpu.SemaphoreType.DMA((len(pieces),))] * 3,
        compiler_params=pltpu.CompilerParams(vmem_limit_bytes=GRANT),
    )(place, mine, other, t_one, t_two, z, kept)


def widen(data, masks, mask, size):
    got = lax.ppermute(data, "col", [(i, i ^ mask) for i in range(size)])
    return got, masks + [m ^ mask for m in masks]


def gather_pieces(own, size):
    unit = own.shape[1] // sum(SHARES)
    sizes = [unit * share for share in SHARES]
    pieces, halves = [], []
    for pair, early_steps, late_steps in ((0, (XA, XB), (YA, YB)), (2, (YA, YB), (XA, XB))):
        base = sum(sizes[:pair])
        data, masks = own[:, base : base + sizes[pair] + sizes[pair + 1]], [0]
        for step in early_steps:
            got, masks = widen(data, masks, step, size)
            data = jnp.concatenate([data, got], 0)
        for i, steps in ((0, late_steps), (1, late_steps[::-1])):
            low = i * sizes[pair]
            part = data[:, low : low + sizes[pair + i]]
            got, held = widen(part, masks, steps[0], size)
            part = jnp.concatenate([part, got], 0)
            got, held = widen(part, held, steps[1], size)
            pieces.append(Piece(base + low, sizes[pair + i], held))
            halves.append((part, got))
    return pieces, halves


def sum_over_row(part):
    r, m = part.shape
    group = PAIRS * NEAR
    rows = group * FAR
    pair = [(i, i ^ 1) for i in range(rows)]
    near = [[group * g + PAIRS * i + c for i in range(NEAR)] for g in range(FAR) for c in range(PAIRS)]
    far = [[i + group * g for g in range(FAR)] for i in range(group)]
    core = lax.axis_index("row") % PAIRS
    half = r // PAIRS
    kept = lax.dynamic_slice_in_dim(part, core * half, half, 0)
    given = lax.dynamic_slice_in_dim(part, (1 - core) * half, half, 0)
    mine = kept + lax.ppermute(given, "row", pair)
    blocks = lax.all_to_all(mine.reshape(NEAR, half // NEAR, m), "row", 0, 0, axis_index_groups=near, tiled=True)
    mine = jnp.sum(blocks, 0)
    blocks = lax.all_to_all(
        jnp.broadcast_to(mine[None], (FAR,) + mine.shape), "row", 0, 0, axis_index_groups=far, tiled=True
    )
    mine = jnp.sum(blocks, 0)
    blocks = lax.all_to_all(
        jnp.broadcast_to(mine[None], (NEAR,) + mine.shape), "row", 0, 0, axis_index_groups=near, tiled=True
    )
    mine = blocks.reshape(half, m)
    return mine, lax.ppermute(mine, "row", pair)


def body(size, z_slab, v_first, v_second, t_first, t_second):
    width = v_first.shape[1]
    k = t_first.shape[0]
    own = lax.optimization_barrier(jnp.concatenate([v_first.T, v_second.T], 0))
    pieces, halves = gather_pieces(own, size)
    place = jnp.stack([lax.axis_index("col"), lax.axis_index("row") % PAIRS]).astype(jnp.int32)
    place = lax.optimization_barrier(place)
    part, z_both, firsts, kept = early(z_slab, [half[0] for half in halves], pieces, k, width)
    for p, piece in enumerate(pieces):
        two = firsts[2 * p : 2 * p + 2]
        part, kept = late(part, halves[p][1], two, z_both, kept, piece, p == 0, k, width)
    mine, other = sum_over_row(part)
    return apply(place, mine, other, t_first, t_second, z_slab, kept, pieces, width)


def solution(mesh):
    placed = (P("row", "col"), P("row", "col"), P("row", "col"), P(), P())
    return jax.shard_map(
        functools.partial(body, mesh.shape["col"]),
        mesh=mesh,
        in_specs=placed,
        out_specs=P("row", "col"),
        check_vma=False,
    )
```

```python
import functools

import jax
import jax.numpy as jnp
from jax import lax
from jax.experimental import pallas as pl
from jax.experimental.pallas import tpu as pltpu
from jax.sharding import PartitionSpec as P

F32 = jnp.float32
BF16 = jnp.bfloat16
XA, XB, YA, YB = 1, 3, 4, 12
SHARES = (7, 5, 7, 5)
PAIRS = 2
NEAR = 4
FAR = 4
GRANT = 32 << 20
PLANES = 6


def dot(left, right):
    return jnp.dot(left, right, preferred_element_type=F32)


def dot_t(left, right):
    return lax.dot_general(left, right, (((1,), (1,)), ((), ())), preferred_element_type=F32)


def split(x):
    high = x.astype(BF16)
    return high, (x - high.astype(F32)).astype(BF16)


def thrice(left, right):
    left_h, left_l = split(left)
    right_h, right_l = split(right)
    return dot(left_h, right_h) + (dot(left_h, right_l) + dot(left_l, right_h))


class Piece:
    def __init__(self, base, size, masks):
        self.base, self.size, self.masks = base, size, masks


def block(place, width, base=0):
    return pl.ds(pl.multiple_of(base + place * width, width), width)


def half_coeffs(high, low, z_both):
    m = z_both.shape[1] // 2
    wide = dot(high, z_both)
    return wide[:, :m] + (wide[:, m:] + dot(low, z_both[:, :m]))


def add_coeffs(out_ref, part, masks, k, width):
    for i, mask in enumerate(masks):
        for which in range(2):
            low, place = (2 * i + which) * width, which * k + mask * width
            out_ref[place : place + width, :] += part[low : low + width, :]


def keep(half, kept, row, base, sem):
    rows, n = half.shape
    copy = pltpu.make_async_copy(half, kept.at[0, pl.ds(row, rows), pl.ds(base, n)], sem)
    copy.start()
    return copy


def early_kernel(pieces, k, width, z_ref, *refs):
    count = len(pieces)
    halves, acc_ref, zb_ref, out = refs[:count], refs[count], refs[count + 1], refs[count + 2 : 3 * count + 2]
    kept, sems = refs[3 * count + 2 :]
    m = z_ref.shape[1]
    acc_ref[...] = jnp.zeros_like(acc_ref)
    copies = []
    for p, piece in enumerate(pieces):
        rows = slice(piece.base, piece.base + piece.size)
        zb_ref[rows, :m], zb_ref[rows, m:] = split(z_ref[rows, :])
        out[2 * p][...], out[2 * p + 1][...] = split(halves[p][...])
        for i in range(2):
            copies.append(keep(out[2 * p + i], kept, 2 * i * k, piece.base, sems.at[2 * p + i]))
        part = half_coeffs(out[2 * p][...], out[2 * p + 1][...], zb_ref[rows, :])
        add_coeffs(acc_ref, part, piece.masks[: len(piece.masks) // 2], k, width)
    for copy in copies:
        copy.wait()


def vmem_specs(count):
    return [pl.BlockSpec(memory_space=pltpu.VMEM)] * count


def any_specs(count):
    return [pl.BlockSpec(memory_space=pl.ANY)] * count


SMEM = [pl.BlockSpec(memory_space=pltpu.SMEM)]


def early(z, halves, pieces, k, width):
    n, m = z.shape
    pairs = [jax.ShapeDtypeStruct(half.shape, BF16) for half in halves for _ in range(2)]
    shapes = [jax.ShapeDtypeStruct((2 * k, m), F32), jax.ShapeDtypeStruct((n, 2 * m), BF16)] + pairs
    out = pl.pallas_call(
        functools.partial(early_kernel, pieces, k, width),
        out_shape=shapes + [jax.ShapeDtypeStruct((PLANES, 4 * k, n), BF16)],
        in_specs=vmem_specs(1 + len(halves)),
        out_specs=vmem_specs(len(shapes)) + any_specs(1),
        scratch_shapes=[pltpu.SemaphoreType.DMA((len(pairs),))],
        compiler_params=pltpu.CompilerParams(vmem_limit_bytes=GRANT),
        cost_estimate=pl.CostEstimate(flops=6 * k * n * m, bytes_accessed=12 << 20, transcendentals=0),
    )(z, *halves)
    return out[0], out[1], out[2:-1], out[-1]


def late_kernel(pieces, k, width, acc_ref, zb_ref, *refs):
    count = len(pieces)
    firsts, gots, out_ref, kept = refs[: 2 * count], refs[2 * count : 3 * count], refs[3 * count + 1], refs[3 * count + 2]
    scratch = refs[3 * count + 3 :]
    raw, pairs, load_sems, sems = scratch[:count], scratch[count : 3 * count], scratch[-2], scratch[-1]
    m = zb_ref.shape[1] // 2
    half = k // (2 * width)
    loads = [pltpu.make_async_copy(gots[p], raw[p], load_sems.at[p]) for p in range(count)]
    for load in loads:
        load.start()
    out_ref[: 2 * k, :] = acc_ref[...]
    copies = []
    for p, piece in enumerate(pieces):
        got = pairs[2 * p : 2 * p + 2]
        loads[p].wait()
        got[0][...], got[1][...] = split(raw[p][...])
        for i in range(2):
            copies.append(keep(got[i], kept, (2 * i + 1) * k, piece.base, sems.at[2 * p + i]))

        def panel(which, i):
            blocks = [None] * (2 * half)
            for pos, mask in enumerate(piece.masks):
                ref, low = (firsts[2 * p + i], got[i])[pos // half], (pos % half * 2 + which) * width
                blocks[mask] = ref[low : low + width, :]
            return jnp.concatenate(blocks, 0)

        part = half_coeffs(got[0][...], got[1][...], zb_ref[piece.base : piece.base + piece.size, :])
        add_coeffs(out_ref, part, piece.masks[half:], k, width)
        one_h, one_l, two_h, two_l = [panel(which, i) for which in range(2) for i in range(2)]
        gram = dot_t(one_h, two_h) + (dot_t(one_h, two_l) + dot_t(one_l, two_h))
        for i in range(k // m):
            rows, part = slice((2 + i) * k, (3 + i) * k), gram[:, i * m : (i + 1) * m]
            out_ref[rows, :] = part if p == 0 else out_ref[rows, :] + part
    for copy in copies:
        copy.wait()


def late(acc, zb, firsts, gots, kept, pieces, k, width):
    m = zb.shape[1] // 2
    count = len(pieces)
    dma = pltpu.SemaphoreType.DMA
    return pl.pallas_call(
        functools.partial(late_kernel, pieces, k, width),
        out_shape=[jax.ShapeDtypeStruct((2 * k + k * k // m, m), F32), jax.ShapeDtypeStruct(kept.shape, BF16)],
        in_specs=vmem_specs(2 + 2 * count) + any_specs(count + 1),
        out_specs=vmem_specs(1) + any_specs(1),
        input_output_aliases={2 + 3 * count: 1},
        scratch_shapes=[pltpu.VMEM(got.shape, F32) for got in gots]
        + [pltpu.VMEM(got.shape, BF16) for got in gots for _ in range(2)]
        + [dma((count,)), dma((2 * count,))],
        compiler_params=pltpu.CompilerParams(vmem_limit_bytes=GRANT),
    )(acc, zb, *firsts, *gots, kept)


def apply_kernel(pieces, width, place_ref, mine_ref, other_ref, t_one_ref, t_two_ref, z_ref, kept_ref, *refs):
    out_ref, held, z_held, out_held, total_ref, x_ref, slot_ref, sems, z_sems, out_sems = refs
    k = t_one_ref.shape[0]
    m = z_ref.shape[1]
    loads, z_loads = [], []
    for p, piece in enumerate(pieces):
        lanes = pl.ds(piece.base, piece.size)
        loads.append(pltpu.make_async_copy(kept_ref.at[0, :, lanes], held.at[:, lanes], sems.at[p]))
        z_loads.append(pltpu.make_async_copy(z_ref.at[lanes, :], z_held.at[lanes, :], z_sems.at[p]))
        loads[p].start()
        z_loads[p].start()
    core = place_ref[1]
    half = mine_ref.shape[0]
    total_ref[block(core, half), :] = mine_ref[...]
    total_ref[block(1 - core, half), :] = other_ref[...]
    col = place_ref[0]

    def solve(t_ref, coeff, row):
        for mask in range(k // width):
            slot_ref[block(lax.bitwise_xor(col, mask), width), :] = coeff[mask * width : (mask + 1) * width, :]
        slot_ref[:k, :] = thrice(t_ref[...], slot_ref[:k, :])
        for mask in range(k // width):
            x_ref[row + mask * width : row + (mask + 1) * width, :] = slot_ref[block(lax.bitwise_xor(col, mask), width), :]

    solve(t_two_ref, total_ref[k : 2 * k, :], k)
    coeff = total_ref[:k, :]
    for i in range(k // m):
        row = (2 + i) * k
        coeff = coeff - thrice(total_ref[row : row + k, :], x_ref[k + i * m : k + (i + 1) * m, :])
    solve(t_one_ref, coeff, 0)
    stores = []
    for p, piece in enumerate(pieces):
        for pos, mask in enumerate(piece.masks):
            for which in range(2):
                low, row = (2 * pos + which) * width, which * k + mask * width
                slot_ref[low : low + width, :] = x_ref[row : row + width, :]
        x_h, x_l = split(slot_ref[...].T)
        x_both = jnp.concatenate([x_h, x_l], 0)
        loads[p].wait()
        z_loads[p].wait()
        rows = slice(piece.base, piece.base + piece.size)
        wide = dot(x_both, held[: 2 * k, rows])
        moved = wide[:m, :] + (wide[m:, :] + dot(x_h, held[2 * k :, rows]))
        out_held[rows, :] = z_held[rows, :] - moved.T
        lanes = pl.ds(piece.base, piece.size)
        stores.append(pltpu.make_async_copy(out_held.at[lanes, :], out_ref.at[lanes, :], out_sems.at[p]))
        stores[-1].start()
    for store in stores:
        store.wait()


def apply(place, mine, other, t_one, t_two, z, kept, pieces, width):
    k, m = t_one.shape[0], z.shape[1]
    rows = pltpu.VMEM(z.shape, F32)
    coeffs = pltpu.VMEM((2 * k, m), F32)
    return pl.pallas_call(
        functools.partial(apply_kernel, pieces, width),
        out_shape=jax.ShapeDtypeStruct(z.shape, F32),
        in_specs=SMEM + vmem_specs(4) + any_specs(2),
        out_specs=pl.BlockSpec(memory_space=pl.ANY),
        scratch_shapes=[pltpu.VMEM(kept.shape[1:], BF16), rows, rows, pltpu.VMEM((2 * mine.shape[0], m), F32)]
        + [coeffs, coeffs]
        + [pltpu.SemaphoreType.DMA((len(pieces),))] * 3,
        compiler_params=pltpu.CompilerParams(vmem_limit_bytes=GRANT),
    )(place, mine, other, t_one, t_two, z, kept)


def widen(data, masks, mask, size):
    got = lax.ppermute(data, "col", [(i, i ^ mask) for i in range(size)])
    return got, masks + [m ^ mask for m in masks]


def gather_pieces(own, size):
    unit = own.shape[1] // sum(SHARES)
    sizes = [unit * share for share in SHARES]
    pieces, halves = [], []
    for pair, early_steps, late_steps in ((0, (XA, XB), (YA, YB)), (2, (YA, YB), (XA, XB))):
        base = sum(sizes[:pair])
        data, masks = own[:, base : base + sizes[pair] + sizes[pair + 1]], [0]
        for step in early_steps:
            got, masks = widen(data, masks, step, size)
            data = jnp.concatenate([data, got], 0)
        for i, steps in ((0, late_steps), (1, late_steps[::-1])):
            low = i * sizes[pair]
            part = data[:, low : low + sizes[pair + i]]
            got, held = widen(part, masks, steps[0], size)
            part = jnp.concatenate([part, got], 0)
            got, held = widen(part, held, steps[1], size)
            pieces.append(Piece(base + low, sizes[pair + i], held))
            halves.append((part, got))
    return pieces, halves


def sum_over_row(part):
    r, m = part.shape
    group = PAIRS * NEAR
    rows = group * FAR
    pair = [(i, i ^ 1) for i in range(rows)]
    near = [[group * g + PAIRS * i + c for i in range(NEAR)] for g in range(FAR) for c in range(PAIRS)]
    far = [[i + group * g for g in range(FAR)] for i in range(group)]
    core = lax.axis_index("row") % PAIRS
    half = r // PAIRS
    kept = lax.dynamic_slice_in_dim(part, core * half, half, 0)
    given = lax.dynamic_slice_in_dim(part, (1 - core) * half, half, 0)
    mine = kept + lax.ppermute(given, "row", pair)
    blocks = lax.all_to_all(mine.reshape(NEAR, half // NEAR, m), "row", 0, 0, axis_index_groups=near, tiled=True)
    mine = jnp.sum(blocks, 0)
    blocks = lax.all_to_all(
        jnp.broadcast_to(mine[None], (FAR,) + mine.shape), "row", 0, 0, axis_index_groups=far, tiled=True
    )
    mine = jnp.sum(blocks, 0)
    blocks = lax.all_to_all(
        jnp.broadcast_to(mine[None], (NEAR,) + mine.shape), "row", 0, 0, axis_index_groups=near, tiled=True
    )
    mine = blocks.reshape(half, m)
    return mine, lax.ppermute(mine, "row", pair)


def body(size, z_slab, v_first, v_second, t_first, t_second):
    width = v_first.shape[1]
    k = t_first.shape[0]
    own = lax.optimization_barrier(jnp.concatenate([v_first.T, v_second.T], 0))
    pieces, halves = gather_pieces(own, size)
    place = jnp.stack([lax.axis_index("col"), lax.axis_index("row") % PAIRS]).astype(jnp.int32)
    place = lax.optimization_barrier(place)
    part, z_both, firsts, kept = early(z_slab, [half[0] for half in halves], pieces, k, width)
    part, kept = late(part, z_both, firsts, [half[1] for half in halves], kept, pieces, k, width)
    mine, other = sum_over_row(part)
    return apply(place, mine, other, t_first, t_second, z_slab, kept, pieces, width)


def solution(mesh):
    placed = (P("row", "col"), P("row", "col"), P("row", "col"), P(), P())
    return jax.shard_map(
        functools.partial(body, mesh.shape["col"]),
        mesh=mesh,
        in_specs=placed,
        out_specs=P("row", "col"),
        check_vma=False,
    )
```

```python
import functools

import jax
import jax.numpy as jnp
from jax import lax
from jax.experimental import pallas as pl
from jax.experimental.pallas import tpu as pltpu
from jax.sharding import PartitionSpec as P

F32 = jnp.float32
BF16 = jnp.bfloat16
XA, XB, YA, YB = 1, 3, 4, 12
RANGES = (14, 10)
PARTS = 2
PAIRS = 2
NEAR = 4
FAR = 4
GRANT = 32 << 20
PLANES = 6


def dot(left, right):
    return jnp.dot(left, right, preferred_element_type=F32)


def dot_t(left, right):
    return lax.dot_general(left, right, (((1,), (1,)), ((), ())), preferred_element_type=F32)


def split(x):
    high = x.astype(BF16)
    return high, (x - high.astype(F32)).astype(BF16)


def thrice(left, right):
    left_h, left_l = split(left)
    right_h, right_l = split(right)
    return dot(left_h, right_h) + (dot(left_h, right_l) + dot(left_l, right_h))


class Piece:
    def __init__(self, panel, base, size, masks):
        self.panel, self.base, self.size, self.masks = panel, base, size, masks


def block(place, width, base=0):
    return pl.ds(pl.multiple_of(base + place * width, width), width)


def half_coeffs(high, low, z_both):
    m = z_both.shape[1] // 2
    wide = dot(high, z_both)
    return wide[:, :m] + (wide[:, m:] + dot(low, z_both[:, :m]))


def add_coeffs(out_ref, part, masks, row, width):
    for i, mask in enumerate(masks):
        place = row + mask * width
        out_ref[place : place + width, :] += part[i * width : (i + 1) * width, :]


def keep(half, kept, row, base, sem):
    rows, n = half.shape
    copy = pltpu.make_async_copy(half, kept.at[0, pl.ds(row, rows), pl.ds(base, n)], sem)
    copy.start()
    return copy


def early_kernel(pieces, k, width, z_ref, *refs):
    count = len(pieces)
    halves, acc_ref, zb_ref, out = refs[:count], refs[count], refs[count + 1], refs[count + 2 : 3 * count + 2]
    kept, sems = refs[3 * count + 2 :]
    m = z_ref.shape[1]
    acc_ref[...] = jnp.zeros_like(acc_ref)
    zb_ref[:, :m], zb_ref[:, m:] = split(z_ref[...])
    copies = []
    for p, piece in enumerate(pieces):
        rows = slice(piece.base, piece.base + piece.size)
        pair = out[2 * p : 2 * p + 2]
        pair[0][...], pair[1][...] = split(halves[p][...])
        for i in range(2):
            copies.append(keep(pair[i], kept, (2 * i + piece.panel) * k, piece.base, sems.at[2 * p + i]))
        part = half_coeffs(pair[0][...], pair[1][...], zb_ref[rows, :])
        add_coeffs(acc_ref, part, piece.masks[: len(piece.masks) // 2], piece.panel * k, width)
    for copy in copies:
        copy.wait()


def vmem_specs(count):
    return [pl.BlockSpec(memory_space=pltpu.VMEM)] * count


def any_specs(count):
    return [pl.BlockSpec(memory_space=pl.ANY)] * count


SMEM = [pl.BlockSpec(memory_space=pltpu.SMEM)]


def early(z, halves, pieces, k, width):
    n, m = z.shape
    pairs = [jax.ShapeDtypeStruct(half.shape, BF16) for half in halves for _ in range(2)]
    shapes = [jax.ShapeDtypeStruct((2 * k, m), F32), jax.ShapeDtypeStruct((n, 2 * m), BF16)] + pairs
    out = pl.pallas_call(
        functools.partial(early_kernel, pieces, k, width),
        out_shape=shapes + [jax.ShapeDtypeStruct((PLANES, 4 * k, n), BF16)],
        in_specs=vmem_specs(1 + len(halves)),
        out_specs=vmem_specs(len(shapes)) + any_specs(1),
        scratch_shapes=[pltpu.SemaphoreType.DMA((len(pairs),))],
        compiler_params=pltpu.CompilerParams(vmem_limit_bytes=GRANT),
        cost_estimate=pl.CostEstimate(flops=6 * k * n * m, bytes_accessed=12 << 20, transcendentals=0),
    )(z, *halves)
    return out[0], out[1], out[2:-1], out[-1]


def late_kernel(pieces, first, k, width, acc_ref, zb_ref, *refs):
    firsts, gots, out_ref, kept = refs[:4], refs[4:6], refs[7], refs[8]
    raw, pairs, load_sems, sems = refs[9:11], refs[11:15], refs[15], refs[16]
    m = zb_ref.shape[1] // 2
    half = k // (2 * width)
    loads = [pltpu.make_async_copy(gots[p], raw[p], load_sems.at[p]) for p in range(2)]
    for load in loads:
        load.start()
    done = acc_ref.shape[0]
    out_ref[:done, :] = acc_ref[...]
    copies, panels = [], []
    for p, piece in enumerate(pieces):
        own, got = firsts[2 * p : 2 * p + 2], pairs[2 * p : 2 * p + 2]
        loads[p].wait()
        got[0][...], got[1][...] = split(raw[p][...])
        for i in range(2):
            row = (2 * i + piece.panel) * k + k // 2
            copies.append(keep(got[i], kept, row, piece.base, sems.at[2 * p + i]))
        part = half_coeffs(got[0][...], got[1][...], zb_ref[piece.base : piece.base + piece.size, :])
        add_coeffs(out_ref, part, piece.masks[half:], piece.panel * k, width)
        for i in range(2):
            blocks = [None] * (2 * half)
            for pos, mask in enumerate(piece.masks):
                ref, low = (own[i], got[i])[pos // half], pos % half * width
                blocks[mask] = ref[low : low + width, :]
            panels.append(jnp.concatenate(blocks, 0))
    one_h, one_l, two_h, two_l = panels
    gram = dot_t(one_h, two_h) + (dot_t(one_h, two_l) + dot_t(one_l, two_h))
    for i in range(k // m):
        rows, part = slice((2 + i) * k, (3 + i) * k), gram[:, i * m : (i + 1) * m]
        out_ref[rows, :] = part if first else out_ref[rows, :] + part
    for copy in copies:
        copy.wait()


def late(acc, zb, firsts, gots, kept, pieces, first, k, width):
    m = zb.shape[1] // 2
    dma = pltpu.SemaphoreType.DMA
    return pl.pallas_call(
        functools.partial(late_kernel, pieces, first, k, width),
        out_shape=[jax.ShapeDtypeStruct((2 * k + k * k // m, m), F32), jax.ShapeDtypeStruct(kept.shape, BF16)],
        in_specs=vmem_specs(6) + any_specs(3),
        out_specs=vmem_specs(1) + any_specs(1),
        input_output_aliases={8: 1},
        scratch_shapes=[pltpu.VMEM(got.shape, F32) for got in gots]
        + [pltpu.VMEM(got.shape, BF16) for got in gots for _ in range(2)]
        + [dma((2,)), dma((4,))],
        compiler_params=pltpu.CompilerParams(vmem_limit_bytes=GRANT),
    )(acc, zb, *firsts, *gots, kept)


def apply_kernel(parts, width, place_ref, mine_ref, other_ref, t_one_ref, t_two_ref, z_ref, kept_ref, *refs):
    out_ref, held, z_held, out_held, total_ref, x_ref, slot_ref, sems, z_sems, out_sems = refs
    k = t_one_ref.shape[0]
    m = z_ref.shape[1]
    loads, z_loads = [], []
    for p, (base, size, _) in enumerate(parts):
        lanes = pl.ds(base, size)
        loads.append(pltpu.make_async_copy(kept_ref.at[0, :, lanes], held.at[:, lanes], sems.at[p]))
        z_loads.append(pltpu.make_async_copy(z_ref.at[lanes, :], z_held.at[lanes, :], z_sems.at[p]))
        loads[p].start()
        z_loads[p].start()
    core = place_ref[1]
    half = mine_ref.shape[0]
    total_ref[block(core, half), :] = mine_ref[...]
    total_ref[block(1 - core, half), :] = other_ref[...]
    col = place_ref[0]

    def solve(t_ref, coeff, row):
        for mask in range(k // width):
            slot_ref[block(lax.bitwise_xor(col, mask), width), :] = coeff[mask * width : (mask + 1) * width, :]
        slot_ref[:k, :] = thrice(t_ref[...], slot_ref[:k, :])
        for mask in range(k // width):
            x_ref[row + mask * width : row + (mask + 1) * width, :] = slot_ref[block(lax.bitwise_xor(col, mask), width), :]

    solve(t_two_ref, total_ref[k : 2 * k, :], k)
    coeff = total_ref[:k, :]
    for i in range(k // m):
        row = (2 + i) * k
        coeff = coeff - thrice(total_ref[row : row + k, :], x_ref[k + i * m : k + (i + 1) * m, :])
    solve(t_one_ref, coeff, 0)
    stores = []
    for p, (base, size, orders) in enumerate(parts):
        if orders is not None:
            for which, masks in enumerate(orders):
                for pos, mask in enumerate(masks):
                    low, row = which * k + pos * width, which * k + mask * width
                    slot_ref[low : low + width, :] = x_ref[row : row + width, :]
            x_h, x_l = split(slot_ref[...].T)
            x_both = jnp.concatenate([x_h, x_l], 0)
        loads[p].wait()
        z_loads[p].wait()
        rows, lanes = slice(base, base + size), pl.ds(base, size)
        wide = dot(x_both, held[: 2 * k, rows])
        moved = wide[:m, :] + (wide[m:, :] + dot(x_h, held[2 * k :, rows]))
        out_held[rows, :] = z_held[rows, :] - moved.T
        stores.append(pltpu.make_async_copy(out_held.at[lanes, :], out_ref.at[lanes, :], out_sems.at[p]))
        stores[-1].start()
    for store in stores:
        store.wait()


def apply(place, mine, other, t_one, t_two, z, kept, parts, width):
    k, m = t_one.shape[0], z.shape[1]
    rows = pltpu.VMEM(z.shape, F32)
    coeffs = pltpu.VMEM((2 * k, m), F32)
    return pl.pallas_call(
        functools.partial(apply_kernel, parts, width),
        out_shape=jax.ShapeDtypeStruct(z.shape, F32),
        in_specs=SMEM + vmem_specs(4) + any_specs(2),
        out_specs=pl.BlockSpec(memory_space=pl.ANY),
        scratch_shapes=[pltpu.VMEM(kept.shape[1:], BF16), rows, rows, pltpu.VMEM((2 * mine.shape[0], m), F32)]
        + [coeffs, coeffs]
        + [pltpu.SemaphoreType.DMA((len(parts),))] * 3,
        compiler_params=pltpu.CompilerParams(vmem_limit_bytes=GRANT),
    )(place, mine, other, t_one, t_two, z, kept)


def widen(data, masks, mask, size):
    got = lax.ppermute(data, "col", [(i, i ^ mask) for i in range(size)])
    return got, masks + [m ^ mask for m in masks]


def gather_pieces(owns, size):
    unit = owns[0].shape[1] // sum(RANGES)
    cut = unit * RANGES[0]
    pieces, halves = [], []
    for panel, early_steps, late_steps in ((0, (XA, XB), (YA, YB)), (1, (YA, YB), (XA, XB))):
        data, masks = owns[panel], [0]
        for step in early_steps:
            got, masks = widen(data, masks, step, size)
            data = jnp.concatenate([data, got], 0)
        for low, high, steps in ((0, cut, late_steps), (cut, data.shape[1], late_steps[::-1])):
            part = data[:, low:high]
            got, held = widen(part, masks, steps[0], size)
            part = jnp.concatenate([part, got], 0)
            got, held = widen(part, held, steps[1], size)
            pieces.append(Piece(panel, low, high - low, held))
            halves.append((part, got))
    return pieces, halves


def sum_over_row(part):
    r, m = part.shape
    group = PAIRS * NEAR
    rows = group * FAR
    pair = [(i, i ^ 1) for i in range(rows)]
    near = [[group * g + PAIRS * i + c for i in range(NEAR)] for g in range(FAR) for c in range(PAIRS)]
    far = [[i + group * g for g in range(FAR)] for i in range(group)]
    core = lax.axis_index("row") % PAIRS
    half = r // PAIRS
    kept = lax.dynamic_slice_in_dim(part, core * half, half, 0)
    given = lax.dynamic_slice_in_dim(part, (1 - core) * half, half, 0)
    mine = kept + lax.ppermute(given, "row", pair)
    blocks = lax.all_to_all(mine.reshape(NEAR, half // NEAR, m), "row", 0, 0, axis_index_groups=near, tiled=True)
    mine = jnp.sum(blocks, 0)
    blocks = lax.all_to_all(
        jnp.broadcast_to(mine[None], (FAR,) + mine.shape), "row", 0, 0, axis_index_groups=far, tiled=True
    )
    mine = jnp.sum(blocks, 0)
    blocks = lax.all_to_all(
        jnp.broadcast_to(mine[None], (NEAR,) + mine.shape), "row", 0, 0, axis_index_groups=near, tiled=True
    )
    mine = blocks.reshape(half, m)
    return mine, lax.ppermute(mine, "row", pair)


def body(size, z_slab, v_first, v_second, t_first, t_second):
    width = v_first.shape[1]
    k = t_first.shape[0]
    pieces, halves = gather_pieces((v_first.T, v_second.T), size)
    place = jnp.stack([lax.axis_index("col"), lax.axis_index("row") % PAIRS]).astype(jnp.int32)
    place = lax.optimization_barrier(place)
    part, z_both, firsts, kept = early(z_slab, [half[0] for half in halves], pieces, k, width)
    parts = []
    for r in range(len(RANGES)):
        both = (r, len(RANGES) + r)
        pair = [pieces[p] for p in both]
        two = [half for p in both for half in firsts[2 * p : 2 * p + 2]]
        part, kept = late(part, z_both, two, [halves[p][1] for p in both], kept, pair, r == 0, k, width)
        step = pair[0].size // PARTS
        parts += [(pair[0].base + i * step, step, None if i else [piece.masks for piece in pair]) for i in range(PARTS)]
    mine, other = sum_over_row(part)
    return apply(place, mine, other, t_first, t_second, z_slab, kept, parts, width)


def solution(mesh):
    placed = (P("row", "col"), P("row", "col"), P("row", "col"), P(), P())
    return jax.shard_map(
        functools.partial(body, mesh.shape["col"]),
        mesh=mesh,
        in_specs=placed,
        out_specs=P("row", "col"),
        check_vma=False,
    )
```

```python
import functools

import jax
import jax.numpy as jnp
from jax import lax
from jax.experimental import pallas as pl
from jax.experimental.pallas import tpu as pltpu
from jax.sharding import PartitionSpec as P

F32 = jnp.float32
BF16 = jnp.bfloat16
XA, XB, YA, YB = 1, 3, 4, 12
RANGES = (12, 12)
STEPS = (((XA, XB, YA, YB), (XB, XA, YB, YA)), ((YA, YB, XA, XB), (YB, YA, XB, XA)))
LANES = 128
PAIRS = 2
NEAR = 4
FAR = 4
GRANT = 32 << 20
PLANES = 6


def dot(left, right):
    return jnp.dot(left, right, preferred_element_type=F32)


def dot_t(left, right):
    return lax.dot_general(left, right, (((1,), (1,)), ((), ())), preferred_element_type=F32)


def split(x):
    high = x.astype(BF16)
    return high, (x - high.astype(F32)).astype(BF16)


def thrice(left, right):
    left_h, left_l = split(left)
    right_h, right_l = split(right)
    return dot(left_h, right_h) + (dot(left_h, right_l) + dot(left_l, right_h))


class Piece:
    def __init__(self, panel, part, base, size, masks):
        self.panel, self.part, self.base, self.size, self.masks = panel, part, base, size, masks


def block(place, width, base=0):
    return pl.ds(pl.multiple_of(base + place * width, width), width)


def half_coeffs(high, low, z_both):
    m = z_both.shape[1] // 2
    wide = dot(high, z_both)
    return wide[:, :m] + (wide[:, m:] + dot(low, z_both[:, :m]))


def add_coeffs(out_ref, part, masks, row, width):
    for i, mask in enumerate(masks):
        place = row + mask * width
        out_ref[place : place + width, :] += part[i * width : (i + 1) * width, :]


def keep(half, kept, row, base, sem):
    rows, n = half.shape
    copy = pltpu.make_async_copy(half, kept.at[0, pl.ds(row, rows), pl.ds(base, n)], sem)
    copy.start()
    return copy


def load_half(place_ref, piece, owns, others, raw, sem):
    own = pltpu.make_async_copy(owns[piece.part].at[0], raw, sem)
    other = pltpu.make_async_copy(others[piece.part], raw, sem)
    pl.when(place_ref[1] == piece.panel)(own.start)
    pl.when(place_ref[1] != piece.panel)(other.start)
    return own


def early_kernel(pieces, k, width, place_ref, z_ref, *refs):
    count = len(pieces)
    owns, others = refs[: count // 2], refs[count // 2 : count]
    acc_ref, kept, sems, load_sems, zb_ref = refs[count : count + 5]
    raw, out = refs[count + 5 : 2 * count + 5], refs[2 * count + 5 :]
    m = z_ref.shape[1]
    loads = [load_half(place_ref, piece, owns, others, raw[p], load_sems.at[p]) for p, piece in enumerate(pieces)]
    acc_ref[...] = jnp.zeros_like(acc_ref)
    zb_ref[:, :m], zb_ref[:, m:] = split(z_ref[...])
    copies = []
    for p, piece in enumerate(pieces):
        rows = slice(piece.base, piece.base + piece.size)
        pair = out[2 * p : 2 * p + 2]
        loads[p].wait()
        pair[0][...], pair[1][...] = split(raw[p][...])
        for i in range(2):
            copies.append(keep(pair[i], kept, (2 * i + piece.panel) * k, piece.base, sems.at[2 * p + i]))
        part = half_coeffs(pair[0][...], pair[1][...], zb_ref[rows, :])
        add_coeffs(acc_ref, part, piece.masks[: len(piece.masks) // 2], piece.panel * k, width)
    for copy in copies:
        copy.wait()


def vmem_specs(count):
    return [pl.BlockSpec(memory_space=pltpu.VMEM)] * count


def any_specs(count):
    return [pl.BlockSpec(memory_space=pl.ANY)] * count


SMEM = [pl.BlockSpec(memory_space=pltpu.SMEM)]


def early(place, z, owns, others, pieces, k, width):
    n, m = z.shape
    raw = [(k // 2, piece.size) for piece in pieces]
    dma = pltpu.SemaphoreType.DMA
    return pl.pallas_call(
        functools.partial(early_kernel, pieces, k, width),
        out_shape=[jax.ShapeDtypeStruct((2 * k, m), F32), jax.ShapeDtypeStruct((PLANES, 4 * k, n), BF16)],
        in_specs=SMEM + vmem_specs(1) + any_specs(len(pieces)),
        out_specs=vmem_specs(1) + any_specs(1),
        scratch_shapes=[dma((2 * len(pieces),)), dma((len(pieces),)), pltpu.VMEM((n, 2 * m), BF16)]
        + [pltpu.VMEM(shape, F32) for shape in raw]
        + [pltpu.VMEM(shape, BF16) for shape in raw for _ in range(2)],
        compiler_params=pltpu.CompilerParams(vmem_limit_bytes=GRANT),
        cost_estimate=pl.CostEstimate(flops=6 * k * n * m, bytes_accessed=12 << 20, transcendentals=0),
    )(place, z, *owns, *others)


def late_kernel(pieces, k, width, place_ref, acc_ref, z_ref, *refs):
    count = len(pieces)
    owns, others, out_ref, kept = refs[: count // 2], refs[count // 2 : count], refs[count + 1], refs[count + 2]
    z_sem, load_sems, first_sems, sems, z_held, zb_ref = refs[count + 3 : count + 9]
    scratch = refs[count + 9 :]
    raw, firsts, pairs = scratch[:count], scratch[count : 3 * count], scratch[3 * count :]
    m = z_ref.shape[1]
    half = k // (2 * width)
    order = [p for r in range(count // 2) for p in (r, count // 2 + r)]
    z_load = pltpu.make_async_copy(z_ref, z_held, z_sem)
    loads, first_loads = {}, {}
    for p in order:
        piece = pieces[p]
        loads[p] = load_half(place_ref, piece, owns, others, raw[p], load_sems.at[p])
        if p == 0:
            z_load.start()
        for i in range(2):
            rows, lanes = pl.ds((2 * i + piece.panel) * k, k // 2), pl.ds(piece.base, piece.size)
            load = pltpu.make_async_copy(kept.at[0, rows, lanes], firsts[2 * p + i], first_sems.at[2 * p + i])
            load.start()
            first_loads[2 * p + i] = load
    out_ref[: 2 * k, :] = acc_ref[...]
    copies, panels = [], []
    for p in order:
        piece, own, got = pieces[p], firsts[2 * p : 2 * p + 2], pairs[2 * p : 2 * p + 2]
        loads[p].wait()
        got[0][...], got[1][...] = split(raw[p][...])
        for i in range(2):
            row = (2 * i + piece.panel) * k + k // 2
            copies.append(keep(got[i], kept, row, piece.base, sems.at[2 * p + i]))
        if p == 0:
            z_load.wait()
            zb_ref[:, :m], zb_ref[:, m:] = split(z_held[...])
        part = half_coeffs(got[0][...], got[1][...], zb_ref[piece.base : piece.base + piece.size, :])
        add_coeffs(out_ref, part, piece.masks[half:], piece.panel * k, width)
        first_loads[2 * p].wait()
        first_loads[2 * p + 1].wait()
        for i in range(2):
            blocks = [None] * (2 * half)
            for pos, mask in enumerate(piece.masks):
                ref, low = (own[i], got[i])[pos // half], pos % half * width
                blocks[mask] = ref[low : low + width, :]
            panels.append(jnp.concatenate(blocks, 0))
        if piece.panel == 1:
            one_h, one_l, two_h, two_l = panels
            panels = []
            gram = dot_t(one_h, two_h) + (dot_t(one_h, two_l) + dot_t(one_l, two_h))
            for i in range(k // m):
                rows, part = slice((2 + i) * k, (3 + i) * k), gram[:, i * m : (i + 1) * m]
                out_ref[rows, :] = part if piece.base == 0 else out_ref[rows, :] + part
    for copy in copies:
        copy.wait()


def late(place, acc, z, owns, others, kept, pieces, k, width):
    n, m = z.shape
    count = len(pieces)
    dma = pltpu.SemaphoreType.DMA
    raw = [(k // 2, piece.size) for piece in pieces]
    pairs = [pltpu.VMEM(shape, BF16) for shape in raw for _ in range(2)]
    return pl.pallas_call(
        functools.partial(late_kernel, pieces, k, width),
        out_shape=[jax.ShapeDtypeStruct((2 * k + k * k // m, m), F32), jax.ShapeDtypeStruct(kept.shape, BF16)],
        in_specs=SMEM + vmem_specs(1) + any_specs(count + 2),
        out_specs=vmem_specs(1) + any_specs(1),
        input_output_aliases={3 + count: 1},
        scratch_shapes=[dma, dma((count,)), dma((2 * count,)), dma((2 * count,))]
        + [pltpu.VMEM((n, m), F32), pltpu.VMEM((n, 2 * m), BF16)]
        + [pltpu.VMEM(shape, F32) for shape in raw]
        + pairs
        + pairs,
        compiler_params=pltpu.CompilerParams(vmem_limit_bytes=GRANT),
    )(place, acc, z, *owns, *others, kept)


def apply_kernel(parts, width, place_ref, mine_ref, other_ref, t_one_ref, t_two_ref, z_ref, kept_ref, *refs):
    out_ref, held, z_held, out_held, total_ref, x_ref, slot_ref, sems, z_sems, out_sems = refs
    k = t_one_ref.shape[0]
    m = z_ref.shape[1]
    loads, z_loads = [], []
    for p, (base, size, _) in enumerate(parts):
        lanes = pl.ds(base, size)
        loads.append(pltpu.make_async_copy(kept_ref.at[0, :, lanes], held.at[:, lanes], sems.at[p]))
        z_loads.append(pltpu.make_async_copy(z_ref.at[lanes, :], z_held.at[lanes, :], z_sems.at[p]))
        loads[p].start()
        z_loads[p].start()
    core = place_ref[1]
    half = mine_ref.shape[0]
    total_ref[block(core, half), :] = mine_ref[...]
    total_ref[block(1 - core, half), :] = other_ref[...]
    col = place_ref[0]

    def solve(t_ref, coeff, row):
        for mask in range(k // width):
            slot_ref[block(lax.bitwise_xor(col, mask), width), :] = coeff[mask * width : (mask + 1) * width, :]
        slot_ref[:k, :] = thrice(t_ref[...], slot_ref[:k, :])
        for mask in range(k // width):
            x_ref[row + mask * width : row + (mask + 1) * width, :] = slot_ref[block(lax.bitwise_xor(col, mask), width), :]

    solve(t_two_ref, total_ref[k : 2 * k, :], k)
    coeff = total_ref[:k, :]
    for i in range(k // m):
        row = (2 + i) * k
        coeff = coeff - thrice(total_ref[row : row + k, :], x_ref[k + i * m : k + (i + 1) * m, :])
    solve(t_one_ref, coeff, 0)
    stores = []
    for p, (base, size, orders) in enumerate(parts):
        if orders is not None:
            for which, masks in enumerate(orders):
                for pos, mask in enumerate(masks):
                    low, row = which * k + pos * width, which * k + mask * width
                    slot_ref[low : low + width, :] = x_ref[row : row + width, :]
            x_h, x_l = split(slot_ref[...].T)
            x_both = jnp.concatenate([x_h, x_l], 0)
        loads[p].wait()
        z_loads[p].wait()
        rows, lanes = slice(base, base + size), pl.ds(base, size)
        wide = dot(x_both, held[: 2 * k, rows])
        moved = wide[:m, :] + (wide[m:, :] + dot(x_h, held[2 * k :, rows]))
        out_held[rows, :] = z_held[rows, :] - moved.T
        stores.append(pltpu.make_async_copy(out_held.at[lanes, :], out_ref.at[lanes, :], out_sems.at[p]))
        stores[-1].start()
    for store in stores:
        store.wait()


def apply(place, mine, other, t_one, t_two, z, kept, parts, width):
    k, m = t_one.shape[0], z.shape[1]
    rows = pltpu.VMEM(z.shape, F32)
    coeffs = pltpu.VMEM((2 * k, m), F32)
    return pl.pallas_call(
        functools.partial(apply_kernel, parts, width),
        out_shape=jax.ShapeDtypeStruct(z.shape, F32),
        in_specs=SMEM + vmem_specs(4) + any_specs(2),
        out_specs=pl.BlockSpec(memory_space=pl.ANY),
        scratch_shapes=[pltpu.VMEM(kept.shape[1:], BF16), rows, rows, pltpu.VMEM((2 * mine.shape[0], m), F32)]
        + [coeffs, coeffs]
        + [pltpu.SemaphoreType.DMA((len(parts),))] * 3,
        compiler_params=pltpu.CompilerParams(vmem_limit_bytes=GRANT),
    )(place, mine, other, t_one, t_two, z, kept)


def exchange(data, masks, rows, cols):
    pairs = [(r * cols + c, r * cols + (c ^ masks[r % PAIRS])) for r in range(rows) for c in range(cols)]
    return lax.ppermute(data, ("row", "col"), pairs)


def swap_cores(data, rows):
    return lax.ppermute(data, "row", [(i, i ^ 1) for i in range(rows)])


def gather_pieces(core, v_one, v_two, rows, cols):
    n = v_one.shape[1]
    cut = n // sum(RANGES) * RANGES[0]
    bounds = ((0, cut), (cut, n))
    stay, leave = jnp.where(core == 0, v_one, v_two), jnp.where(core == 0, v_two, v_one)
    stay, leave = lax.optimization_barrier((stay, leave))
    both = jnp.stack([stay, swap_cores(leave, rows)])
    parts = [both[:, :, low:high] for low, high in bounds]
    pieces = [[None] * len(parts) for _ in range(PAIRS)]
    masks = [[[0] for _ in parts] for _ in range(PAIRS)]
    gots = [None] * len(parts)
    for step in range(len(STEPS[0][0])):
        for r in range(len(parts)):
            if step:
                parts[r] = jnp.concatenate([parts[r], gots[r]], 1)
            steps = [STEPS[panel][r][step] for panel in range(PAIRS)]
            gots[r] = exchange(parts[r], steps, rows, cols)
            for panel in range(PAIRS):
                masks[panel][r] = masks[panel][r] + [m ^ steps[panel] for m in masks[panel][r]]
    for panel in range(PAIRS):
        for r, (low, high) in enumerate(bounds):
            pieces[panel][r] = Piece(panel, r, low, high - low, masks[panel][r])
    return pieces[0] + pieces[1], parts, gots


def sum_over_row(part):
    r, m = part.shape
    group = PAIRS * NEAR
    rows = group * FAR
    pair = [(i, i ^ 1) for i in range(rows)]
    near = [[group * g + PAIRS * i + c for i in range(NEAR)] for g in range(FAR) for c in range(PAIRS)]
    far = [[i + group * g for g in range(FAR)] for i in range(group)]
    core = lax.axis_index("row") % PAIRS
    half = r // PAIRS
    kept = lax.dynamic_slice_in_dim(part, core * half, half, 0)
    given = lax.dynamic_slice_in_dim(part, (1 - core) * half, half, 0)
    mine = kept + lax.ppermute(given, "row", pair)
    blocks = lax.all_to_all(mine.reshape(NEAR, half // NEAR, m), "row", 0, 0, axis_index_groups=near, tiled=True)
    mine = jnp.sum(blocks, 0)
    blocks = lax.all_to_all(
        jnp.broadcast_to(mine[None], (FAR,) + mine.shape), "row", 0, 0, axis_index_groups=far, tiled=True
    )
    mine = jnp.sum(blocks, 0)
    blocks = lax.all_to_all(
        jnp.broadcast_to(mine[None], (NEAR,) + mine.shape), "row", 0, 0, axis_index_groups=near, tiled=True
    )
    mine = blocks.reshape(half, m)
    return mine, lax.ppermute(mine, "row", pair)


def body(sizes, z_slab, v_first, v_second, t_first, t_second):
    width = v_first.shape[1]
    k = t_first.shape[0]
    core = lax.axis_index("row") % PAIRS
    pieces, halves, gots = gather_pieces(core, v_first.T, v_second.T, *sizes)
    place = lax.optimization_barrier(jnp.stack([lax.axis_index("col"), core]).astype(jnp.int32))
    others = [swap_cores(half[1], sizes[0]) for half in halves]
    part, kept = early(place, z_slab, halves, others, pieces, k, width)
    gots = [lax.optimization_barrier((part, got))[1] for got in gots]
    others = [swap_cores(half[1], sizes[0]) for half in gots]
    part, kept = late(place, part, z_slab, gots, others, kept, pieces, k, width)
    parts = []
    for r in range(len(RANGES)):
        pair = [pieces[r], pieces[len(RANGES) + r]]
        base, end = pair[0].base, pair[0].base + pair[0].size
        middle = base + -(-pair[0].size // (2 * LANES)) * LANES
        parts += [(base, middle - base, [piece.masks for piece in pair]), (middle, end - middle, None)]
    mine, other = sum_over_row(part)
    return apply(place, mine, other, t_first, t_second, z_slab, kept, parts, width)


def solution(mesh):
    placed = (P("row", "col"), P("row", "col"), P("row", "col"), P(), P())
    return jax.shard_map(
        functools.partial(body, (mesh.shape["row"], mesh.shape["col"])),
        mesh=mesh,
        in_specs=placed,
        out_specs=P("row", "col"),
        check_vma=False,
    )
```

```python
import functools

import jax
import jax.numpy as jnp
from jax import lax
from jax.experimental import pallas as pl
from jax.experimental.pallas import tpu as pltpu
from jax.sharding import PartitionSpec as P

F32 = jnp.float32
BF16 = jnp.bfloat16
XA, XB, YA, YB = 1, 3, 4, 12
SHARES = (7, 5, 7, 5)
ORDER = ((0, 1), (2, 3))
PAIRS = 2
NEAR = 4
FAR = 4
GRANT = 32 << 20
PLANES = 6


def dot(left, right):
    return jnp.dot(left, right, preferred_element_type=F32)


def dot_t(left, right):
    return lax.dot_general(left, right, (((1,), (1,)), ((), ())), preferred_element_type=F32)


def split(x):
    high = x.astype(BF16)
    return high, (x - high.astype(F32)).astype(BF16)


def thrice(left, right):
    left_h, left_l = split(left)
    right_h, right_l = split(right)
    return dot(left_h, right_h) + (dot(left_h, right_l) + dot(left_l, right_h))


class Piece:
    def __init__(self, base, size, masks):
        self.base, self.size, self.masks = base, size, masks


def block(place, width, base=0):
    return pl.ds(pl.multiple_of(base + place * width, width), width)


def half_coeffs(high, low, z_both):
    m = z_both.shape[1] // 2
    wide = dot(high, z_both)
    return wide[:, :m] + (wide[:, m:] + dot(low, z_both[:, :m]))


def add_coeffs(out_ref, part, masks, k, width):
    for i, mask in enumerate(masks):
        for which in range(2):
            low, place = (2 * i + which) * width, which * k + mask * width
            out_ref[place : place + width, :] += part[low : low + width, :]


def keep(half, kept, row, base, sem):
    rows, n = half.shape
    copy = pltpu.make_async_copy(half, kept.at[0, pl.ds(row, rows), pl.ds(base, n)], sem)
    copy.start()
    return copy


def early_kernel(pieces, k, width, z_ref, *refs):
    count = len(pieces)
    halves, acc_ref, zb_ref, out = refs[:count], refs[count], refs[count + 1], refs[count + 2 : 3 * count + 2]
    kept, sems = refs[3 * count + 2 :]
    m = z_ref.shape[1]
    acc_ref[...] = jnp.zeros_like(acc_ref)
    copies = []
    for p, piece in enumerate(pieces):
        rows = slice(piece.base, piece.base + piece.size)
        zb_ref[rows, :m], zb_ref[rows, m:] = split(z_ref[rows, :])
        out[2 * p][...], out[2 * p + 1][...] = split(halves[p][...])
        for i in range(2):
            copies.append(keep(out[2 * p + i], kept, 2 * i * k, piece.base, sems.at[2 * p + i]))
        part = half_coeffs(out[2 * p][...], out[2 * p + 1][...], zb_ref[rows, :])
        add_coeffs(acc_ref, part, piece.masks[: len(piece.masks) // 2], k, width)
    for copy in copies:
        copy.wait()


def vmem_specs(count):
    return [pl.BlockSpec(memory_space=pltpu.VMEM)] * count


def any_specs(count):
    return [pl.BlockSpec(memory_space=pl.ANY)] * count


SMEM = [pl.BlockSpec(memory_space=pltpu.SMEM)]


def early(z, halves, pieces, k, width):
    n, m = z.shape
    pairs = [jax.ShapeDtypeStruct(half.shape, BF16) for half in halves for _ in range(2)]
    shapes = [jax.ShapeDtypeStruct((2 * k, m), F32), jax.ShapeDtypeStruct((n, 2 * m), BF16)] + pairs
    out = pl.pallas_call(
        functools.partial(early_kernel, pieces, k, width),
        out_shape=shapes + [jax.ShapeDtypeStruct((PLANES, 4 * k, n), BF16)],
        in_specs=vmem_specs(1 + len(halves)),
        out_specs=vmem_specs(len(shapes)) + any_specs(1),
        scratch_shapes=[pltpu.SemaphoreType.DMA((len(pairs),))],
        compiler_params=pltpu.CompilerParams(vmem_limit_bytes=GRANT),
        cost_estimate=pl.CostEstimate(flops=6 * k * n * m, bytes_accessed=12 << 20, transcendentals=0),
    )(z, *halves)
    return out[0], out[1], out[2:-1], out[-1]


def late_kernel(pieces, first, k, width, acc_ref, zb_ref, *refs):
    count = len(pieces)
    firsts, gots, out_ref, kept = refs[: 2 * count], refs[2 * count : 3 * count], refs[3 * count + 1], refs[3 * count + 2]
    scratch = refs[3 * count + 3 :]
    raw, pairs, load_sems, sems = scratch[:count], scratch[count : 3 * count], scratch[-2], scratch[-1]
    m = zb_ref.shape[1] // 2
    half = k // (2 * width)
    loads = [pltpu.make_async_copy(gots[p], raw[p], load_sems.at[p]) for p in range(count)]
    for load in loads:
        load.start()
    done = acc_ref.shape[0]
    out_ref[:done, :] = acc_ref[...]
    copies = []
    for p, piece in enumerate(pieces):
        got = pairs[2 * p : 2 * p + 2]
        loads[p].wait()
        got[0][...], got[1][...] = split(raw[p][...])
        for i in range(2):
            copies.append(keep(got[i], kept, (2 * i + 1) * k, piece.base, sems.at[2 * p + i]))

        def panel(which, i):
            blocks = [None] * (2 * half)
            for pos, mask in enumerate(piece.masks):
                ref, low = (firsts[2 * p + i], got[i])[pos // half], (pos % half * 2 + which) * width
                blocks[mask] = ref[low : low + width, :]
            return jnp.concatenate(blocks, 0)

        part = half_coeffs(got[0][...], got[1][...], zb_ref[piece.base : piece.base + piece.size, :])
        add_coeffs(out_ref, part, piece.masks[half:], k, width)
        one_h, one_l, two_h, two_l = [panel(which, i) for which in range(2) for i in range(2)]
        gram = dot_t(one_h, two_h) + (dot_t(one_h, two_l) + dot_t(one_l, two_h))
        for i in range(k // m):
            rows, part = slice((2 + i) * k, (3 + i) * k), gram[:, i * m : (i + 1) * m]
            out_ref[rows, :] = part if first and p == 0 else out_ref[rows, :] + part
    for copy in copies:
        copy.wait()


def late(acc, zb, firsts, gots, kept, pieces, first, k, width):
    m = zb.shape[1] // 2
    count = len(pieces)
    dma = pltpu.SemaphoreType.DMA
    return pl.pallas_call(
        functools.partial(late_kernel, pieces, first, k, width),
        out_shape=[jax.ShapeDtypeStruct((2 * k + k * k // m, m), F32), jax.ShapeDtypeStruct(kept.shape, BF16)],
        in_specs=vmem_specs(2 + 2 * count) + any_specs(count + 1),
        out_specs=vmem_specs(1) + any_specs(1),
        input_output_aliases={2 + 3 * count: 1},
        scratch_shapes=[pltpu.VMEM(got.shape, F32) for got in gots]
        + [pltpu.VMEM(got.shape, BF16) for got in gots for _ in range(2)]
        + [dma((count,)), dma((2 * count,))],
        compiler_params=pltpu.CompilerParams(vmem_limit_bytes=GRANT),
    )(acc, zb, *firsts, *gots, kept)


def apply_kernel(pieces, width, place_ref, mine_ref, other_ref, t_one_ref, t_two_ref, z_ref, kept_ref, *refs):
    out_ref, held, z_held, out_held, total_ref, x_ref, slot_ref, sems, z_sems, out_sems = refs
    k = t_one_ref.shape[0]
    m = z_ref.shape[1]
    loads, z_loads = [], []
    for p, piece in enumerate(pieces):
        lanes = pl.ds(piece.base, piece.size)
        loads.append(pltpu.make_async_copy(kept_ref.at[0, :, lanes], held.at[:, lanes], sems.at[p]))
        z_loads.append(pltpu.make_async_copy(z_ref.at[lanes, :], z_held.at[lanes, :], z_sems.at[p]))
        loads[p].start()
        z_loads[p].start()
    core = place_ref[1]
    half = mine_ref.shape[0]
    total_ref[block(core, half), :] = mine_ref[...]
    total_ref[block(1 - core, half), :] = other_ref[...]
    col = place_ref[0]

    def solve(t_ref, coeff, row):
        for mask in range(k // width):
            slot_ref[block(lax.bitwise_xor(col, mask), width), :] = coeff[mask * width : (mask + 1) * width, :]
        slot_ref[:k, :] = thrice(t_ref[...], slot_ref[:k, :])
        for mask in range(k // width):
            x_ref[row + mask * width : row + (mask + 1) * width, :] = slot_ref[block(lax.bitwise_xor(col, mask), width), :]

    solve(t_two_ref, total_ref[k : 2 * k, :], k)
    coeff = total_ref[:k, :]
    for i in range(k // m):
        row = (2 + i) * k
        coeff = coeff - thrice(total_ref[row : row + k, :], x_ref[k + i * m : k + (i + 1) * m, :])
    solve(t_one_ref, coeff, 0)
    stores = []
    for p, piece in enumerate(pieces):
        for pos, mask in enumerate(piece.masks):
            for which in range(2):
                low, row = (2 * pos + which) * width, which * k + mask * width
                slot_ref[low : low + width, :] = x_ref[row : row + width, :]
        x_h, x_l = split(slot_ref[...].T)
        x_both = jnp.concatenate([x_h, x_l], 0)
        loads[p].wait()
        z_loads[p].wait()
        rows = slice(piece.base, piece.base + piece.size)
        wide = dot(x_both, held[: 2 * k, rows])
        moved = wide[:m, :] + (wide[m:, :] + dot(x_h, held[2 * k :, rows]))
        out_held[rows, :] = z_held[rows, :] - moved.T
        lanes = pl.ds(piece.base, piece.size)
        stores.append(pltpu.make_async_copy(out_held.at[lanes, :], out_ref.at[lanes, :], out_sems.at[p]))
        stores[-1].start()
    for store in stores:
        store.wait()


def apply(place, mine, other, t_one, t_two, z, kept, pieces, width):
    k, m = t_one.shape[0], z.shape[1]
    rows = pltpu.VMEM(z.shape, F32)
    coeffs = pltpu.VMEM((2 * k, m), F32)
    return pl.pallas_call(
        functools.partial(apply_kernel, pieces, width),
        out_shape=jax.ShapeDtypeStruct(z.shape, F32),
        in_specs=SMEM + vmem_specs(4) + any_specs(2),
        out_specs=pl.BlockSpec(memory_space=pl.ANY),
        scratch_shapes=[pltpu.VMEM(kept.shape[1:], BF16), rows, rows, pltpu.VMEM((2 * mine.shape[0], m), F32)]
        + [coeffs, coeffs]
        + [pltpu.SemaphoreType.DMA((len(pieces),))] * 3,
        compiler_params=pltpu.CompilerParams(vmem_limit_bytes=GRANT),
    )(place, mine, other, t_one, t_two, z, kept)


def widen(data, masks, mask, size):
    got = lax.ppermute(data, "col", [(i, i ^ mask) for i in range(size)])
    return got, masks + [m ^ mask for m in masks]


def gather_pieces(own, size):
    unit = own.shape[1] // sum(SHARES)
    sizes = [unit * share for share in SHARES]
    pieces, halves = [], []
    for pair, early_steps, late_steps in ((0, (XA, XB), (YA, YB)), (2, (YA, YB), (XA, XB))):
        base = sum(sizes[:pair])
        data, masks = own[:, base : base + sizes[pair] + sizes[pair + 1]], [0]
        for step in early_steps:
            got, masks = widen(data, masks, step, size)
            data = jnp.concatenate([data, got], 0)
        for i, steps in ((0, late_steps), (1, late_steps[::-1])):
            low = i * sizes[pair]
            part = data[:, low : low + sizes[pair + i]]
            got, held = widen(part, masks, steps[0], size)
            part = jnp.concatenate([part, got], 0)
            got, held = widen(part, held, steps[1], size)
            pieces.append(Piece(base + low, sizes[pair + i], held))
            halves.append((part, got))
    return pieces, halves


def sum_over_row(part):
    r, m = part.shape
    group = PAIRS * NEAR
    rows = group * FAR
    pair = [(i, i ^ 1) for i in range(rows)]
    near = [[group * g + PAIRS * i + c for i in range(NEAR)] for g in range(FAR) for c in range(PAIRS)]
    far = [[i + group * g for g in range(FAR)] for i in range(group)]
    core = lax.axis_index("row") % PAIRS
    half = r // PAIRS
    kept = lax.dynamic_slice_in_dim(part, core * half, half, 0)
    given = lax.dynamic_slice_in_dim(part, (1 - core) * half, half, 0)
    mine = kept + lax.ppermute(given, "row", pair)
    blocks = lax.all_to_all(mine.reshape(NEAR, half // NEAR, m), "row", 0, 0, axis_index_groups=near, tiled=True)
    mine = jnp.sum(blocks, 0)
    blocks = lax.all_to_all(
        jnp.broadcast_to(mine[None], (FAR,) + mine.shape), "row", 0, 0, axis_index_groups=far, tiled=True
    )
    mine = jnp.sum(blocks, 0)
    blocks = lax.all_to_all(
        jnp.broadcast_to(mine[None], (NEAR,) + mine.shape), "row", 0, 0, axis_index_groups=near, tiled=True
    )
    mine = blocks.reshape(half, m)
    return mine, lax.ppermute(mine, "row", pair)


def body(size, z_slab, v_first, v_second, t_first, t_second):
    width = v_first.shape[1]
    k = t_first.shape[0]
    own = lax.optimization_barrier(jnp.concatenate([v_first.T, v_second.T], 0))
    pieces, halves = gather_pieces(own, size)
    place = jnp.stack([lax.axis_index("col"), lax.axis_index("row") % PAIRS]).astype(jnp.int32)
    place = lax.optimization_barrier(place)
    part, z_both, firsts, kept = early(z_slab, [half[0] for half in halves], pieces, k, width)
    for pair in ORDER:
        two = [half for p in pair for half in firsts[2 * p : 2 * p + 2]]
        some, gots = [pieces[p] for p in pair], [halves[p][1] for p in pair]
        part, kept = late(part, z_both, two, gots, kept, some, pair == ORDER[0], k, width)
    mine, other = sum_over_row(part)
    return apply(place, mine, other, t_first, t_second, z_slab, kept, pieces, width)


def solution(mesh):
    placed = (P("row", "col"), P("row", "col"), P("row", "col"), P(), P())
    return jax.shard_map(
        functools.partial(body, mesh.shape["col"]),
        mesh=mesh,
        in_specs=placed,
        out_specs=P("row", "col"),
        check_vma=False,
    )
```

```python
import functools

import jax
import jax.numpy as jnp
from jax import lax
from jax.experimental import pallas as pl
from jax.experimental.pallas import tpu as pltpu
from jax.sharding import PartitionSpec as P

F32 = jnp.float32
BF16 = jnp.bfloat16
XA, XB, YA, YB = 1, 3, 4, 12
SHARES = (7, 5, 7, 5)
ORDER = ((0, 1), (2, 3))
PAIRS = 2
NEAR = 4
FAR = 4
GRANT = 32 << 20
PLANES = 6


def dot(left, right):
    return jnp.dot(left, right, preferred_element_type=F32)


def dot_t(left, right):
    return lax.dot_general(left, right, (((1,), (1,)), ((), ())), preferred_element_type=F32)


def split(x):
    high = x.astype(BF16)
    return high, (x - high.astype(F32)).astype(BF16)


def thrice(left, right):
    left_h, left_l = split(left)
    right_h, right_l = split(right)
    return dot(left_h, right_h) + (dot(left_h, right_l) + dot(left_l, right_h))


class Piece:
    def __init__(self, base, size, masks):
        self.base, self.size, self.masks = base, size, masks


def block(place, width, base=0):
    return pl.ds(pl.multiple_of(base + place * width, width), width)


def half_coeffs(high, low, z_both):
    m = z_both.shape[1] // 2
    wide = dot(high, z_both)
    return wide[:, :m] + (wide[:, m:] + dot(low, z_both[:, :m]))


def add_coeffs(out_ref, part, masks, k, width):
    for i, mask in enumerate(masks):
        for which in range(2):
            low, place = (2 * i + which) * width, which * k + mask * width
            out_ref[place : place + width, :] += part[low : low + width, :]


def keep(half, kept, row, base, sem):
    rows, n = half.shape
    copy = pltpu.make_async_copy(half, kept.at[0, pl.ds(row, rows), pl.ds(base, n)], sem)
    copy.start()
    return copy


def early_kernel(pieces, k, width, z_ref, *refs):
    count = len(pieces)
    halves, acc_ref, zb_ref, out = refs[:count], refs[count], refs[count + 1], refs[count + 2 : 3 * count + 2]
    kept, sems = refs[3 * count + 2 :]
    m = z_ref.shape[1]
    acc_ref[...] = jnp.zeros_like(acc_ref)
    copies = []
    for p, piece in enumerate(pieces):
        rows = slice(piece.base, piece.base + piece.size)
        zb_ref[rows, :m], zb_ref[rows, m:] = split(z_ref[rows, :])
        out[2 * p][...], out[2 * p + 1][...] = split(halves[p][...])
        for i in range(2):
            copies.append(keep(out[2 * p + i], kept, 2 * i * k, piece.base, sems.at[2 * p + i]))
        part = half_coeffs(out[2 * p][...], out[2 * p + 1][...], zb_ref[rows, :])
        add_coeffs(acc_ref, part, piece.masks[: len(piece.masks) // 2], k, width)
    for copy in copies:
        copy.wait()


def vmem_specs(count):
    return [pl.BlockSpec(memory_space=pltpu.VMEM)] * count


def any_specs(count):
    return [pl.BlockSpec(memory_space=pl.ANY)] * count


SMEM = [pl.BlockSpec(memory_space=pltpu.SMEM)]


def early(z, halves, pieces, k, width):
    n, m = z.shape
    pairs = [jax.ShapeDtypeStruct(half.shape, BF16) for half in halves for _ in range(2)]
    shapes = [jax.ShapeDtypeStruct((2 * k, m), F32), jax.ShapeDtypeStruct((n, 2 * m), BF16)] + pairs
    out = pl.pallas_call(
        functools.partial(early_kernel, pieces, k, width),
        out_shape=shapes + [jax.ShapeDtypeStruct((PLANES, 4 * k, n), BF16)],
        in_specs=vmem_specs(1 + len(halves)),
        out_specs=vmem_specs(len(shapes)) + any_specs(1),
        scratch_shapes=[pltpu.SemaphoreType.DMA((len(pairs),))],
        compiler_params=pltpu.CompilerParams(vmem_limit_bytes=GRANT),
        cost_estimate=pl.CostEstimate(flops=6 * k * n * m, bytes_accessed=12 << 20, transcendentals=0),
    )(z, *halves)
    return out[0], out[1], out[2:-1], out[-1]


def late_kernel(pieces, first, k, width, acc_ref, zb_ref, *refs):
    count = len(pieces)
    firsts, gots, out_ref, kept = refs[: 2 * count], refs[2 * count : 3 * count], refs[3 * count + 1], refs[3 * count + 2]
    scratch = refs[3 * count + 3 :]
    raw, pairs, load_sems, sems = scratch[:count], scratch[count : 3 * count], scratch[-2], scratch[-1]
    m = zb_ref.shape[1] // 2
    half = k // (2 * width)
    loads = [pltpu.make_async_copy(gots[p], raw[p], load_sems.at[p]) for p in range(count)]
    for load in loads:
        load.start()
    done = acc_ref.shape[0]
    out_ref[:done, :] = acc_ref[...]
    copies = []
    for p, piece in enumerate(pieces):
        got = pairs[2 * p : 2 * p + 2]
        loads[p].wait()
        got[0][...], got[1][...] = split(raw[p][...])
        for i in range(2):
            copies.append(keep(got[i], kept, (2 * i + 1) * k, piece.base, sems.at[2 * p + i]))

        def panel(which, i):
            blocks = [None] * (2 * half)
            for pos, mask in enumerate(piece.masks):
                ref, low = (firsts[2 * p + i], got[i])[pos // half], (pos % half * 2 + which) * width
                blocks[mask] = ref[low : low + width, :]
            return jnp.concatenate(blocks, 0)

        part = half_coeffs(got[0][...], got[1][...], zb_ref[piece.base : piece.base + piece.size, :])
        add_coeffs(out_ref, part, piece.masks[half:], k, width)
        one_h, one_l, two_h, two_l = [panel(which, i) for which in range(2) for i in range(2)]
        gram = dot_t(one_h, two_h) + (dot_t(one_h, two_l) + dot_t(one_l, two_h))
        for i in range(k // m):
            rows, part = slice((2 + i) * k, (3 + i) * k), gram[:, i * m : (i + 1) * m]
            out_ref[rows, :] = part if first and p == 0 else out_ref[rows, :] + part
    for copy in copies:
        copy.wait()


def late(acc, zb, firsts, gots, kept, pieces, first, k, width):
    m = zb.shape[1] // 2
    count = len(pieces)
    dma = pltpu.SemaphoreType.DMA
    return pl.pallas_call(
        functools.partial(late_kernel, pieces, first, k, width),
        out_shape=[jax.ShapeDtypeStruct((2 * k + k * k // m, m), F32), jax.ShapeDtypeStruct(kept.shape, BF16)],
        in_specs=vmem_specs(2 + 2 * count) + any_specs(count + 1),
        out_specs=vmem_specs(1) + any_specs(1),
        input_output_aliases={2 + 3 * count: 1},
        scratch_shapes=[pltpu.VMEM(got.shape, F32) for got in gots]
        + [pltpu.VMEM(got.shape, BF16) for got in gots for _ in range(2)]
        + [dma((count,)), dma((2 * count,))],
        compiler_params=pltpu.CompilerParams(vmem_limit_bytes=GRANT),
    )(acc, zb, *firsts, *gots, kept)


def apply_kernel(pieces, width, place_ref, mine_ref, other_ref, t_one_ref, t_two_ref, z_ref, kept_ref, *refs):
    out_ref, held, out_held, total_ref, x_ref, slot_ref, sems, out_sems = refs
    k = t_one_ref.shape[0]
    m = z_ref.shape[1]
    loads = []
    for p, piece in enumerate(pieces):
        lanes = pl.ds(piece.base, piece.size)
        loads.append(pltpu.make_async_copy(kept_ref.at[0, :, lanes], held.at[:, lanes], sems.at[p]))
        loads[p].start()
    core = place_ref[1]
    half = mine_ref.shape[0]
    total_ref[block(core, half), :] = mine_ref[...]
    total_ref[block(1 - core, half), :] = other_ref[...]
    col = place_ref[0]

    def solve(t_ref, coeff, row):
        for mask in range(k // width):
            slot_ref[block(lax.bitwise_xor(col, mask), width), :] = coeff[mask * width : (mask + 1) * width, :]
        slot_ref[:k, :] = thrice(t_ref[...], slot_ref[:k, :])
        for mask in range(k // width):
            x_ref[row + mask * width : row + (mask + 1) * width, :] = slot_ref[block(lax.bitwise_xor(col, mask), width), :]

    solve(t_two_ref, total_ref[k : 2 * k, :], k)
    gram = jnp.concatenate([total_ref[(2 + i) * k : (3 + i) * k, :] for i in range(k // m)], 1)
    coeff = total_ref[:k, :] - thrice(gram, x_ref[k:, :])
    solve(t_one_ref, coeff, 0)
    stores = []
    for p, piece in enumerate(pieces):
        for pos, mask in enumerate(piece.masks):
            for which in range(2):
                low, row = (2 * pos + which) * width, which * k + mask * width
                slot_ref[low : low + width, :] = x_ref[row : row + width, :]
        x_h, x_l = split(slot_ref[...].T)
        x_both = jnp.concatenate([x_h, x_l], 0)
        loads[p].wait()
        rows = slice(piece.base, piece.base + piece.size)
        wide = dot(x_both, held[: 2 * k, rows])
        moved = wide[:m, :] + (wide[m:, :] + dot(x_h, held[2 * k :, rows]))
        out_held[rows, :] = z_ref[rows, :] - moved.T
        lanes = pl.ds(piece.base, piece.size)
        stores.append(pltpu.make_async_copy(out_held.at[lanes, :], out_ref.at[lanes, :], out_sems.at[p]))
        stores[-1].start()
    for store in stores:
        store.wait()


def apply(place, mine, other, t_one, t_two, z, kept, pieces, width):
    k, m = t_one.shape[0], z.shape[1]
    rows = pltpu.VMEM(z.shape, F32)
    coeffs = pltpu.VMEM((2 * k, m), F32)
    return pl.pallas_call(
        functools.partial(apply_kernel, pieces, width),
        out_shape=jax.ShapeDtypeStruct(z.shape, F32),
        in_specs=SMEM + vmem_specs(5) + any_specs(1),
        out_specs=pl.BlockSpec(memory_space=pl.ANY),
        scratch_shapes=[pltpu.VMEM(kept.shape[1:], BF16), rows, pltpu.VMEM((2 * mine.shape[0], m), F32)]
        + [coeffs, coeffs]
        + [pltpu.SemaphoreType.DMA((len(pieces),))] * 2,
        compiler_params=pltpu.CompilerParams(vmem_limit_bytes=GRANT),
    )(place, mine, other, t_one, t_two, z, kept)


def widen(data, masks, mask, size):
    got = lax.ppermute(data, "col", [(i, i ^ mask) for i in range(size)])
    return got, masks + [m ^ mask for m in masks]


def gather_pieces(own, size):
    unit = own.shape[1] // sum(SHARES)
    sizes = [unit * share for share in SHARES]
    pieces, halves = [], []
    for pair, early_steps, late_steps in ((0, (XA, XB), (YA, YB)), (2, (YA, YB), (XA, XB))):
        base = sum(sizes[:pair])
        data, masks = own[:, base : base + sizes[pair] + sizes[pair + 1]], [0]
        for step in early_steps:
            got, masks = widen(data, masks, step, size)
            data = jnp.concatenate([data, got], 0)
        for i, steps in ((0, late_steps), (1, late_steps[::-1])):
            low = i * sizes[pair]
            part = data[:, low : low + sizes[pair + i]]
            got, held = widen(part, masks, steps[0], size)
            part = jnp.concatenate([part, got], 0)
            got, held = widen(part, held, steps[1], size)
            pieces.append(Piece(base + low, sizes[pair + i], held))
            halves.append((part, got))
    return pieces, halves


def sum_over_row(part):
    r, m = part.shape
    group = PAIRS * NEAR
    rows = group * FAR
    pair = [(i, i ^ 1) for i in range(rows)]
    near = [[group * g + PAIRS * i + c for i in range(NEAR)] for g in range(FAR) for c in range(PAIRS)]
    far = [[i + group * g for g in range(FAR)] for i in range(group)]
    core = lax.axis_index("row") % PAIRS
    half = r // PAIRS
    kept = lax.dynamic_slice_in_dim(part, core * half, half, 0)
    given = lax.dynamic_slice_in_dim(part, (1 - core) * half, half, 0)
    mine = kept + lax.ppermute(given, "row", pair)
    blocks = lax.all_to_all(mine.reshape(NEAR, half // NEAR, m), "row", 0, 0, axis_index_groups=near, tiled=True)
    mine = jnp.sum(blocks, 0)
    blocks = lax.all_to_all(
        jnp.broadcast_to(mine[None], (FAR,) + mine.shape), "row", 0, 0, axis_index_groups=far, tiled=True
    )
    mine = jnp.sum(blocks, 0)
    blocks = lax.all_to_all(
        jnp.broadcast_to(mine[None], (NEAR,) + mine.shape), "row", 0, 0, axis_index_groups=near, tiled=True
    )
    mine = blocks.reshape(half, m)
    return mine, lax.ppermute(mine, "row", pair)


def body(size, z_slab, v_first, v_second, t_first, t_second):
    width = v_first.shape[1]
    k = t_first.shape[0]
    own = lax.optimization_barrier(jnp.concatenate([v_first.T, v_second.T], 0))
    pieces, halves = gather_pieces(own, size)
    place = jnp.stack([lax.axis_index("col"), lax.axis_index("row") % PAIRS]).astype(jnp.int32)
    place = lax.optimization_barrier(place)
    part, z_both, firsts, kept = early(z_slab, [half[0] for half in halves], pieces, k, width)
    for pair in ORDER:
        two = [half for p in pair for half in firsts[2 * p : 2 * p + 2]]
        some, gots = [pieces[p] for p in pair], [halves[p][1] for p in pair]
        part, kept = late(part, z_both, two, gots, kept, some, pair == ORDER[0], k, width)
    mine, other = sum_over_row(part)
    return apply(place, mine, other, t_first, t_second, z_slab, kept, pieces, width)


def solution(mesh):
    placed = (P("row", "col"), P("row", "col"), P("row", "col"), P(), P())
    return jax.shard_map(
        functools.partial(body, mesh.shape["col"]),
        mesh=mesh,
        in_specs=placed,
        out_specs=P("row", "col"),
        check_vma=False,
    )
```

```python
import functools

import jax
import jax.numpy as jnp
from jax import lax
from jax.experimental import pallas as pl
from jax.experimental.pallas import tpu as pltpu
from jax.sharding import PartitionSpec as P

F32 = jnp.float32
BF16 = jnp.bfloat16
XA, XB, YA, YB = 1, 3, 4, 12
SHARES = (7, 5, 7, 5)
ORDER = ((0, 1), (2, 3))
PAIRS = 2
NEAR = 4
FAR = 4
GRANT = 32 << 20
PLANES = 6


def dot(left, right):
    return jnp.dot(left, right, preferred_element_type=F32)


def dot_t(left, right):
    return lax.dot_general(left, right, (((1,), (1,)), ((), ())), preferred_element_type=F32)


def split(x):
    high = x.astype(BF16)
    return high, (x - high.astype(F32)).astype(BF16)


def thrice(left, right):
    left_h, left_l = split(left)
    right_h, right_l = split(right)
    return dot(left_h, right_h) + (dot(left_h, right_l) + dot(left_l, right_h))


class Piece:
    def __init__(self, base, size, masks):
        self.base, self.size, self.masks = base, size, masks


def block(place, width, base=0):
    return pl.ds(pl.multiple_of(base + place * width, width), width)


def half_coeffs(high, low, z_both):
    m = z_both.shape[1] // 2
    wide = dot(high, z_both)
    return wide[:, :m] + (wide[:, m:] + dot(low, z_both[:, :m]))


def add_coeffs(out_ref, part, masks, k, width):
    for i, mask in enumerate(masks):
        for which in range(2):
            low, place = (2 * i + which) * width, which * k + mask * width
            out_ref[place : place + width, :] += part[low : low + width, :]


def keep(half, kept, row, base, sem):
    rows, n = half.shape
    copy = pltpu.make_async_copy(half, kept.at[0, pl.ds(row, rows), pl.ds(base, n)], sem)
    copy.start()
    return copy


def early_kernel(pieces, k, width, z_ref, *refs):
    count = len(pieces)
    halves, acc_ref, zb_ref, out = refs[:count], refs[count], refs[count + 1], refs[count + 2 : 3 * count + 2]
    kept, sems = refs[3 * count + 2 :]
    m = z_ref.shape[1]
    acc_ref[...] = jnp.zeros_like(acc_ref)
    copies = []
    for p, piece in enumerate(pieces):
        rows = slice(piece.base, piece.base + piece.size)
        zb_ref[rows, :m], zb_ref[rows, m:] = split(z_ref[rows, :])
        out[2 * p][...], out[2 * p + 1][...] = split(halves[p][...])
        for i in range(2):
            copies.append(keep(out[2 * p + i], kept, 2 * i * k, piece.base, sems.at[2 * p + i]))
        part = half_coeffs(out[2 * p][...], out[2 * p + 1][...], zb_ref[rows, :])
        add_coeffs(acc_ref, part, piece.masks[: len(piece.masks) // 2], k, width)
    for copy in copies:
        copy.wait()


def vmem_specs(count):
    return [pl.BlockSpec(memory_space=pltpu.VMEM)] * count


def any_specs(count):
    return [pl.BlockSpec(memory_space=pl.ANY)] * count


SMEM = [pl.BlockSpec(memory_space=pltpu.SMEM)]


def early(z, halves, pieces, k, width):
    n, m = z.shape
    pairs = [jax.ShapeDtypeStruct(half.shape, BF16) for half in halves for _ in range(2)]
    shapes = [jax.ShapeDtypeStruct((2 * k, m), F32), jax.ShapeDtypeStruct((n, 2 * m), BF16)] + pairs
    out = pl.pallas_call(
        functools.partial(early_kernel, pieces, k, width),
        out_shape=shapes + [jax.ShapeDtypeStruct((PLANES, 4 * k, n), BF16)],
        in_specs=vmem_specs(1 + len(halves)),
        out_specs=vmem_specs(len(shapes)) + any_specs(1),
        scratch_shapes=[pltpu.SemaphoreType.DMA((len(pairs),))],
        compiler_params=pltpu.CompilerParams(vmem_limit_bytes=GRANT),
        cost_estimate=pl.CostEstimate(flops=6 * k * n * m, bytes_accessed=12 << 20, transcendentals=0),
    )(z, *halves)
    return out[0], out[1], out[2:-1], out[-1]


def late_kernel(pieces, first, k, width, acc_ref, zb_ref, *refs):
    count = len(pieces)
    firsts, gots, out_ref, kept = refs[: 2 * count], refs[2 * count : 3 * count], refs[3 * count + 1], refs[3 * count + 2]
    scratch = refs[3 * count + 3 :]
    raw, pairs, load_sems, sems = scratch[:count], scratch[count : 3 * count], scratch[-2], scratch[-1]
    m = zb_ref.shape[1] // 2
    half = k // (2 * width)
    loads = [pltpu.make_async_copy(gots[p], raw[p], load_sems.at[p]) for p in range(count)]
    for load in loads:
        load.start()
    done = acc_ref.shape[0]
    out_ref[:done, :] = acc_ref[...]
    copies = []
    for p, piece in enumerate(pieces):
        got = pairs[2 * p : 2 * p + 2]
        loads[p].wait()
        got[0][...], got[1][...] = split(raw[p][...])
        for i in range(2):
            copies.append(keep(got[i], kept, (2 * i + 1) * k, piece.base, sems.at[2 * p + i]))

        def panel(which, i):
            blocks = [None] * (2 * half)
            for pos, mask in enumerate(piece.masks):
                ref, low = (firsts[2 * p + i], got[i])[pos // half], (pos % half * 2 + which) * width
                blocks[mask] = ref[low : low + width, :]
            return jnp.concatenate(blocks, 0)

        part = half_coeffs(got[0][...], got[1][...], zb_ref[piece.base : piece.base + piece.size, :])
        add_coeffs(out_ref, part, piece.masks[half:], k, width)
        one_h, one_l, two_h, two_l = [panel(which, i) for which in range(2) for i in range(2)]
        gram = dot_t(one_h, two_h) + (dot_t(one_h, two_l) + dot_t(one_l, two_h))
        for i in range(k // m):
            rows, part = slice((2 + i) * k, (3 + i) * k), gram[:, i * m : (i + 1) * m]
            out_ref[rows, :] = part if first and p == 0 else out_ref[rows, :] + part
    for copy in copies:
        copy.wait()


def late(acc, zb, firsts, gots, kept, pieces, first, k, width):
    m = zb.shape[1] // 2
    count = len(pieces)
    dma = pltpu.SemaphoreType.DMA
    return pl.pallas_call(
        functools.partial(late_kernel, pieces, first, k, width),
        out_shape=[jax.ShapeDtypeStruct((2 * k + k * k // m, m), F32), jax.ShapeDtypeStruct(kept.shape, BF16)],
        in_specs=vmem_specs(2 + 2 * count) + any_specs(count + 1),
        out_specs=vmem_specs(1) + any_specs(1),
        input_output_aliases={2 + 3 * count: 1},
        scratch_shapes=[pltpu.VMEM(got.shape, F32) for got in gots]
        + [pltpu.VMEM(got.shape, BF16) for got in gots for _ in range(2)]
        + [dma((count,)), dma((2 * count,))],
        compiler_params=pltpu.CompilerParams(vmem_limit_bytes=GRANT),
    )(acc, zb, *firsts, *gots, kept)


def apply_kernel(pieces, width, place_ref, mine_ref, other_ref, t_both, z_ref, kept_ref, *refs):
    out_ref, held, z_held, out_held, total_ref, x_ref, slot_ref, sems, z_sems, out_sems = refs
    t_one_ref, t_two_ref = t_both.at[0], t_both.at[1]
    k = t_both.shape[1]
    m = z_ref.shape[1]
    loads, z_loads = [], []
    for p, piece in enumerate(pieces):
        lanes = pl.ds(piece.base, piece.size)
        loads.append(pltpu.make_async_copy(kept_ref.at[0, :, lanes], held.at[:, lanes], sems.at[p]))
        z_loads.append(pltpu.make_async_copy(z_ref.at[lanes, :], z_held.at[lanes, :], z_sems.at[p]))
        loads[p].start()
        z_loads[p].start()
    core = place_ref[1]
    half = mine_ref.shape[0]
    total_ref[block(core, half), :] = mine_ref[...]
    total_ref[block(1 - core, half), :] = other_ref[...]
    col = place_ref[0]

    def solve(t_ref, coeff, row):
        for mask in range(k // width):
            slot_ref[block(lax.bitwise_xor(col, mask), width), :] = coeff[mask * width : (mask + 1) * width, :]
        slot_ref[:k, :] = thrice(t_ref[...], slot_ref[:k, :])
        for mask in range(k // width):
            x_ref[row + mask * width : row + (mask + 1) * width, :] = slot_ref[block(lax.bitwise_xor(col, mask), width), :]

    solve(t_two_ref, total_ref[k : 2 * k, :], k)
    coeff = total_ref[:k, :]
    for i in range(k // m):
        row = (2 + i) * k
        coeff = coeff - thrice(total_ref[row : row + k, :], x_ref[k + i * m : k + (i + 1) * m, :])
    solve(t_one_ref, coeff, 0)
    stores = []
    for p, piece in enumerate(pieces):
        for pos, mask in enumerate(piece.masks):
            for which in range(2):
                low, row = (2 * pos + which) * width, which * k + mask * width
                slot_ref[low : low + width, :] = x_ref[row : row + width, :]
        x_h, x_l = split(slot_ref[...].T)
        x_both = jnp.concatenate([x_h, x_l], 0)
        loads[p].wait()
        z_loads[p].wait()
        rows = slice(piece.base, piece.base + piece.size)
        wide = dot(x_both, held[: 2 * k, rows])
        moved = wide[:m, :] + (wide[m:, :] + dot(x_h, held[2 * k :, rows]))
        out_held[rows, :] = z_held[rows, :] - moved.T
        lanes = pl.ds(piece.base, piece.size)
        stores.append(pltpu.make_async_copy(out_held.at[lanes, :], out_ref.at[lanes, :], out_sems.at[p]))
        stores[-1].start()
    for store in stores:
        store.wait()


def apply(place, mine, other, t_both, z, kept, pieces, width):
    k, m = t_both.shape[1], z.shape[1]
    rows = pltpu.VMEM(z.shape, F32)
    coeffs = pltpu.VMEM((2 * k, m), F32)
    return pl.pallas_call(
        functools.partial(apply_kernel, pieces, width),
        out_shape=jax.ShapeDtypeStruct(z.shape, F32),
        in_specs=SMEM + vmem_specs(3) + any_specs(2),
        out_specs=pl.BlockSpec(memory_space=pl.ANY),
        scratch_shapes=[pltpu.VMEM(kept.shape[1:], BF16), rows, rows, pltpu.VMEM((2 * mine.shape[0], m), F32)]
        + [coeffs, coeffs]
        + [pltpu.SemaphoreType.DMA((len(pieces),))] * 3,
        compiler_params=pltpu.CompilerParams(vmem_limit_bytes=GRANT),
    )(place, mine, other, t_both, z, kept)


def widen(data, masks, mask, size):
    got = lax.ppermute(data, "col", [(i, i ^ mask) for i in range(size)])
    return got, masks + [m ^ mask for m in masks]


def gather_pieces(own, size):
    unit = own.shape[1] // sum(SHARES)
    sizes = [unit * share for share in SHARES]
    pieces, halves = [], []
    for pair, early_steps, late_steps in ((0, (XA, XB), (YA, YB)), (2, (YA, YB), (XA, XB))):
        base = sum(sizes[:pair])
        data, masks = own[:, base : base + sizes[pair] + sizes[pair + 1]], [0]
        for step in early_steps:
            got, masks = widen(data, masks, step, size)
            data = jnp.concatenate([data, got], 0)
        for i, steps in ((0, late_steps), (1, late_steps[::-1])):
            low = i * sizes[pair]
            part = data[:, low : low + sizes[pair + i]]
            got, held = widen(part, masks, steps[0], size)
            part = jnp.concatenate([part, got], 0)
            got, held = widen(part, held, steps[1], size)
            pieces.append(Piece(base + low, sizes[pair + i], held))
            halves.append((part, got))
    return pieces, halves


def sum_over_row(part):
    r, m = part.shape
    group = PAIRS * NEAR
    rows = group * FAR
    pair = [(i, i ^ 1) for i in range(rows)]
    near = [[group * g + PAIRS * i + c for i in range(NEAR)] for g in range(FAR) for c in range(PAIRS)]
    far = [[i + group * g for g in range(FAR)] for i in range(group)]
    core = lax.axis_index("row") % PAIRS
    half = r // PAIRS
    kept = lax.dynamic_slice_in_dim(part, core * half, half, 0)
    given = lax.dynamic_slice_in_dim(part, (1 - core) * half, half, 0)
    mine = kept + lax.ppermute(given, "row", pair)
    blocks = lax.all_to_all(mine.reshape(NEAR, half // NEAR, m), "row", 0, 0, axis_index_groups=near, tiled=True)
    mine = jnp.sum(blocks, 0)
    blocks = lax.all_to_all(
        jnp.broadcast_to(mine[None], (FAR,) + mine.shape), "row", 0, 0, axis_index_groups=far, tiled=True
    )
    mine = jnp.sum(blocks, 0)
    blocks = lax.all_to_all(
        jnp.broadcast_to(mine[None], (NEAR,) + mine.shape), "row", 0, 0, axis_index_groups=near, tiled=True
    )
    mine = blocks.reshape(half, m)
    return mine, lax.ppermute(mine, "row", pair)


def body(size, z_slab, v_first, v_second, t_first, t_second):
    width = v_first.shape[1]
    k = t_first.shape[0]
    own = lax.optimization_barrier(jnp.concatenate([v_first.T, v_second.T], 0))
    pieces, halves = gather_pieces(own, size)
    place = jnp.stack([lax.axis_index("col"), lax.axis_index("row") % PAIRS]).astype(jnp.int32)
    place = lax.optimization_barrier(place)
    part, z_both, firsts, kept = early(z_slab, [half[0] for half in halves], pieces, k, width)
    for pair in ORDER:
        two = [half for p in pair for half in firsts[2 * p : 2 * p + 2]]
        some, gots = [pieces[p] for p in pair], [halves[p][1] for p in pair]
        part, kept = late(part, z_both, two, gots, kept, some, pair == ORDER[0], k, width)
    t_both = lax.optimization_barrier(jnp.stack([t_first, t_second]))
    mine, other = sum_over_row(part)
    return apply(place, mine, other, t_both, z_slab, kept, pieces, width)


def solution(mesh):
    placed = (P("row", "col"), P("row", "col"), P("row", "col"), P(), P())
    return jax.shard_map(
        functools.partial(body, mesh.shape["col"]),
        mesh=mesh,
        in_specs=placed,
        out_specs=P("row", "col"),
        check_vma=False,
    )
```
